512 devices in a mesh: seq: 16 (over y, core), table: 32 (over z, x).
Axes of the slice: x: 4, y: 8, z: 8, core: 2. Of those that a mesh axis runs over, the one named last changes fastest.
Arguments:
- table: bfloat16 [32768, 512], P('table'), may hold values from -6 to 6
- item_rows: int32 [32, 2048], P('table', 'seq'), may hold values from 0 to 32767, as said below
- lengths: int32 [32], P('table'), may hold values from 512 to 2048, as said below
- w_in: bfloat16 [512, 2048], replicated, may hold values from -0.25 to 0.25
- w_out: bfloat16 [512, 512], replicated, may hold values from -0.25 to 0.25
- cotangent: bfloat16 [32, 2048, 512], P('table', 'seq'), may hold values from -6 to 6
Outputs:
- table_grad: float32 [32768, 512], P('table', 'seq')
- w_out_grad: float32 [512, 512], P('table')
The draws below stay inside these ranges and needn't reach their ends.
Inputs may be any that keep to these rules, and one draw needn't show every extreme that they name: `item_rows`: A row's owner is its index divided by 1024. The 128 events of one device name rows of at most 8 events for each owner; in every draw one owner gets exactly 8 events from every device of a group along table. `lengths`: in every draw some user's history is live in all 2048 positions.
All inputs are finite; a program needn't handle non-finite values.
Results may differ from the reference program's by a relative error of at most 0.025.
Values may be sent and summed in bfloat16 or wider, within the bound.
A program may use at most 128 MiB of HBM per device.

```python
import jax
import jax.numpy as jnp
from jax import lax

D = 512
HEADS = 8
ROWS_T = 1024
TOK_DEV = 128
L = 2048
USERS = 32
ROWS = 32768
CAP = 8
N_SEQ = 16
N_TABLE = 32


def draw_item_rows(key, part):
    key = jax.random.fold_in(key, 11)
    first, second, third = jax.random.split(key, 3)
    offset = jax.random.randint(first, (), 0, N_TABLE)
    busiest_owner = (offset + jnp.arange(N_SEQ)) % N_TABLE
    block_busiest = jnp.tile(busiest_owner, USERS)
    others = jnp.arange((N_TABLE - 1) * CAP) // CAP

    def one_block(block_key, busiest):
        pick_key, order_key = jax.random.split(block_key)
        shifted = others + (others >= busiest).astype(others.dtype)
        chosen = jax.random.permutation(pick_key, shifted)[:TOK_DEV - CAP]
        owners = jnp.concatenate([jnp.full((CAP,), busiest, jnp.int32), chosen.astype(jnp.int32)])
        return jax.random.permutation(order_key, owners)
    block_keys = jax.random.split(second, USERS * N_SEQ)
    flat_owner = jax.vmap(one_block)(block_keys, block_busiest).reshape(-1)
    flat_local = jax.random.randint(third, (USERS * L,), 0, ROWS_T)
    indices = jnp.arange(USERS * L)
    last_place = jnp.argmax(flat_owner == N_TABLE - 1)
    first_place = jnp.argmax(flat_owner == 0)
    flat_local = jnp.where(indices == last_place, ROWS_T - 1, flat_local)
    flat_local = jnp.where(indices == first_place, 0, flat_local)
    return (flat_owner * ROWS_T + flat_local).reshape(USERS, L).astype(jnp.int32)


def draw_lengths(key, part):
    key = jax.random.fold_in(key, 23)
    first, second = jax.random.split(key)
    drawn = jax.random.randint(first, (USERS,), L // 4, L + 1)
    full_user = jax.random.randint(second, (), 0, USERS)
    return jnp.where(jnp.arange(USERS) == full_user, L, drawn).astype(jnp.int32)


def shard_levels(stream_key, shape, cuts, least, high):
    level = 1.0
    for position, shards_of in cuts:
        draws = jax.random.uniform(jax.random.fold_in(jax.random.fold_in(stream_key, 6), position), (shards_of,), jnp.float32, least / len(cuts), high / len(cuts))
        level = level * jnp.repeat(jnp.exp(draws), shape[position] // shards_of).reshape((-1,) + (1,) * (len(shape) - 1 - position))
    return level


def scatter_about(key, shape, scale, most, cuts=(), kind=jnp.bfloat16):
    gain = shard_levels(key, shape, cuts, -0.22, 0.18) if cuts else 1.0
    values = jax.random.normal(key, shape, jnp.float32) * scale * gain
    return jnp.minimum(jnp.maximum(values, -most), most).astype(kind)


def setup_inputs(seed: int = 0) -> dict:
    key_list = jax.random.split(jax.random.key(seed), 7)
    return {
        "table": scatter_about(key_list[0], (ROWS, D), 1.0, 6.0, ((0, 32),)),
        "item_rows": draw_item_rows(jax.random.fold_in(key_list[6], 71), 0),
        "lengths": draw_lengths(jax.random.fold_in(key_list[6], 71), 0),
        "w_in": scatter_about(key_list[3], (D, 4 * D), D ** -0.5, 0.25),
        "w_out": scatter_about(key_list[4], (D, D), D ** -0.5, 0.25),
        "cotangent": scatter_about(key_list[5], (USERS, L, D), 1.0, 6.0, ((0, 32), (1, 16))),
    }


EPS = 1e-05

def positions(index):
    block = index // TOK_DEV
    within = index % TOK_DEV
    half = TOK_DEV // 2
    span = jnp.where(within < half, block, 2 * N_SEQ - 1 - block)
    return (span * half + within % half).astype(jnp.int32)

def normalize(values):
    center = values - lax.optimization_barrier(jnp.mean(values, axis=-1, keepdims=True))
    scale_inv = lax.rsqrt(lax.optimization_barrier(jnp.mean(center * center, axis=-1, keepdims=True)) + EPS)
    return (center * scale_inv, scale_inv)

def norm_back(grad, normed, scale_inv):
    first = lax.optimization_barrier(jnp.mean(grad, axis=-1, keepdims=True))
    second = lax.optimization_barrier(jnp.mean(grad * normed, axis=-1, keepdims=True))
    return scale_inv * (grad - first - normed * second)

def silu_slope(values):
    sigma = jax.nn.sigmoid(values)
    return sigma * (1.0 + values * (1.0 - sigma))

def reference(table, item_rows, lengths, w_in, w_out, cotangent):
    head_size = D // HEADS
    factor = head_size ** (-0.5)
    place = positions(jnp.arange(L, dtype=jnp.int32))

    def split_heads(part):
        return part.reshape(L, HEADS, head_size).transpose(1, 0, 2)

    def join_heads(part):
        return part.transpose(1, 0, 2).reshape(L, D)

    def one_user(inputs):
        rows, length, grad_out = inputs
        is_live = place < length
        visible = (place[None, :] <= place[:, None]) & is_live[None, :]
        embedded = table[rows]
        normed_f, inv_first = normalize(embedded.astype(jnp.float32))
        normed = normed_f.astype(jnp.bfloat16)
        before = jnp.dot(normed, w_in, preferred_element_type=jnp.float32)
        projected = jax.nn.silu(before).astype(jnp.bfloat16)
        gate_u = projected[:, :D]
        values = split_heads(projected[:, D:2 * D])
        queries = split_heads(projected[:, 2 * D:3 * D])
        keys = split_heads(projected[:, 3 * D:])

        def head_forward(parts):
            query, key, value = parts
            score = jnp.dot(query, key.T, preferred_element_type=jnp.float32) * factor
            weight = jnp.where(visible, jax.nn.silu(score), 0.0).astype(jnp.bfloat16)
            return jnp.dot(weight, value, preferred_element_type=jnp.float32)
        attended = join_heads(lax.map(head_forward, (queries, keys, values)))
        normed_y, inv_second = normalize(attended)
        mixed = (normed_y * gate_u.astype(jnp.float32)).astype(jnp.bfloat16)
        grad = jnp.where(is_live[:, None], grad_out, jnp.zeros_like(grad_out))
        weight_grad = jnp.dot(mixed.T, grad, preferred_element_type=jnp.float32)
        grad_mixed = jnp.dot(grad, w_out.T, preferred_element_type=jnp.float32)
        grad_gate = grad_mixed * normed_y
        grad_attended = norm_back(grad_mixed * gate_u.astype(jnp.float32), normed_y, inv_second).astype(jnp.bfloat16)

        def head_backward(parts):
            query, key, value, grad_head = parts
            score = jnp.dot(query, key.T, preferred_element_type=jnp.float32) * factor
            weight = jnp.where(visible, jax.nn.silu(score), 0.0).astype(jnp.bfloat16)
            grad_weight = jnp.dot(grad_head, value.T, preferred_element_type=jnp.float32)
            grad_score = jnp.where(visible, grad_weight * silu_slope(score), 0.0).astype(jnp.bfloat16)
            grad_query = jnp.dot(grad_score, key, preferred_element_type=jnp.float32) * factor
            grad_key = jnp.dot(grad_score.T, query, preferred_element_type=jnp.float32) * factor
            grad_value = jnp.dot(weight.T, grad_head, preferred_element_type=jnp.float32)
            return (grad_query, grad_key, grad_value)
        grad_q, grad_k, grad_v = lax.map(head_backward, (queries, keys, values, split_heads(grad_attended)))
        grad_proj = jnp.concatenate([grad_gate, join_heads(grad_v), join_heads(grad_q), join_heads(grad_k)], axis=1)
        grad_before = (grad_proj * silu_slope(before)).astype(jnp.bfloat16)
        grad_normed = jnp.dot(grad_before, w_in.T, preferred_element_type=jnp.float32)
        grad_rows = grad.astype(jnp.float32) + norm_back(grad_normed, normed_f, inv_first)
        return (grad_rows, weight_grad)
    grad_rows, weight_grads = lax.map(one_user, (item_rows, lengths, cotangent))
    table_grad = jax.ops.segment_sum(grad_rows.reshape(-1, D), item_rows.reshape(-1), num_segments=ROWS)
    return (table_grad, lax.optimization_barrier(jnp.sum(weight_grads, axis=0)))
```

```python
import jax
import jax.numpy as jnp
from jax import lax
from jax.experimental import pallas as pl
from jax.experimental.pallas import tpu as pltpu
from jax.sharding import PartitionSpec as P

EPS = 1e-05
MESH = pl.DeviceIdType.MESH
F32 = jnp.float32
BF16 = jnp.bfloat16
I32 = jnp.int32

N_SEQ = 16
N_TABLE = 32
EVENTS = 128
WIDTH = 512
HEADS = 8
HEAD = 64
CAP = 8
ROWS_T = 1024
SLOTS = N_TABLE * CAP
HIDDEN = -64.0


def mm(a, b):
    return jnp.dot(a, b, preferred_element_type=F32)


def mm_t(a, b):
    return lax.dot_general(a, b, (((1,), (1,)), ((), ())), preferred_element_type=F32)


def iota(shape, dim):
    return lax.broadcasted_iota(I32, shape, dim)


def one_hot(mask):
    return jnp.where(mask, 1.0, 0.0).astype(BF16)


def swap(tile):
    return pltpu.roll(tile, 64, tile.ndim - 1)


def left(shape):
    return iota(shape, len(shape) - 1) < 64


def kernel(
    rows_ref,
    len_ref,
    cot_ref,
    table_hbm,
    w_in_hbm,
    w_out_hbm,
    out_ref,
    w_grad_ref,
    table_v,
    w_in_v,
    w_out_v,
    ids_send,
    ids_land,
    fetch_send,
    fetch_land,
    slot_send,
    slot_land,
    qkv_send,
    qkv_land,
    kv_sib,
    e_send,
    e_land,
    stat_send,
    stat_land,
    ny_send,
    ny_land,
    w_send,
    w_land,
    part_send,
    part_land,
    sib_send,
    sib_land,
    back_send,
    back_land,
    dx_send,
    dx_land,
    col_send,
    col_land,
    grad_s,
    dz_t,
    u_t,
    nx_s,
    slope_s,
    kv_nat,
    kv_t,
    q_pad,
    dy_pad,
    a_t,
    g_t,
    y_t,
    dq_t,
    dkv_s,
    hot_hi,
    mask_lo,
    load_sem,
    send_sem,
    recv_sem,
    qkv_sem,
):
    me_s = lax.axis_index("seq")
    me_t = lax.axis_index("table")
    y = me_s // 2
    core = me_s % 2
    sibling = me_s + 1 - 2 * core

    loads = [
        pltpu.make_async_copy(src, dst, load_sem.at[k])
        for k, (src, dst) in enumerate(
            ((table_hbm, table_v), (w_out_hbm, w_out_v), (w_in_hbm, w_in_v))
        )
    ]
    for load in loads:
        load.start()

    barrier = pltpu.get_barrier_semaphore()

    def greet_table(d, carry):
        pl.semaphore_signal(
            barrier, inc=1, device_id={"table": (me_t + d) % N_TABLE}, device_id_type=MESH
        )
        return carry

    def greet_seq(d, carry):
        pl.semaphore_signal(
            barrier, inc=1, device_id={"seq": (me_s + d) % N_SEQ}, device_id_type=MESH
        )
        return carry

    lax.fori_loop(1, N_TABLE, greet_table, 0)
    lax.fori_loop(1, N_SEQ, greet_seq, 0)

    def remote(src, dst, k, where, recv=None):
        return pltpu.make_async_remote_copy(
            src_ref=src,
            dst_ref=dst,
            send_sem=send_sem.at[k],
            recv_sem=recv_sem.at[k] if recv is None else recv,
            device_id=where,
            device_id_type=MESH,
        )

    def to_table(src, dst, k, split):
        def body(d, carry):
            peer = (me_t + d) % N_TABLE
            remote(src.at[peer] if split else src, dst.at[me_t], k, {"table": peer}).start()
            return carry

        lax.fori_loop(1, N_TABLE, body, 0)

    def to_seq(src, dst, k, split):
        def body(d, carry):
            peer = (me_s + d) % N_SEQ
            remote(src.at[peer] if split else src, dst.at[me_s], k, {"seq": peer}).start()
            return carry

        lax.fori_loop(1, N_SEQ, body, 0)

    def to_heads(src, dst, k, split, sems=None):
        def body(d, carry):
            peer = (y + d) % HEADS
            recv = None if sems is None else sems.at[y]
            remote(
                src.at[peer] if split else src, dst.at[y], k, {"seq": 2 * peer + core}, recv
            ).start()
            return carry

        lax.fori_loop(1, HEADS, body, 0)

    def wait_recv(ref, k):
        pltpu.make_async_copy(ref, ref, recv_sem.at[k]).wait()

    def wait_sent(ref, k):
        pltpu.make_async_copy(ref, ref, send_sem.at[k]).wait()

    ids_row = rows_ref[...]
    ids_own = jnp.broadcast_to(ids_row, (8, EVENTS))
    ids_send[...] = ids_own
    ids_land[me_t] = ids_own
    pl.semaphore_wait(barrier, N_TABLE - 1 + N_SEQ - 1)
    to_table(ids_send, ids_land, 0, False)

    square = (EVENTS, EVENTS)
    row_of, col_of = iota(square, 0), iota(square, 1)
    ids_wide = jnp.broadcast_to(ids_row, square)
    ids_col = jnp.sum(
        jnp.where(row_of == col_of, ids_wide.astype(F32), 0.0), axis=1, keepdims=True
    ).astype(I32)
    owner_row = ids_wide >> 10
    owner_col = jnp.broadcast_to(ids_col >> 10, square)
    same = owner_row == owner_col
    rank_col = jnp.sum(
        jnp.where(same & (col_of < row_of), 1.0, 0.0), axis=1, keepdims=True
    ).astype(I32)
    rank_row = jnp.sum(
        jnp.where(same & (row_of < col_of), 1.0, 0.0), axis=0, keepdims=True
    ).astype(I32)
    slot_col = (ids_col >> 10) * 16 + rank_col
    slot_row = (ids_row >> 10) * CAP + rank_row

    half = iota((EVENTS, 1), 0)
    span = jnp.where(half < 64, me_s, 2 * N_SEQ - 1 - me_s)
    live = (span * 64 + (half & 63)) < len_ref[0]
    grad = jnp.where(live, cot_ref[...].astype(F32), 0.0)
    grad_b = grad.astype(BF16)
    grad_s[...] = grad
    loads[1].wait()
    dz_t[...] = mm_t(w_out_v[...], grad_b)

    wait_recv(ids_land.at[pl.ds(0, N_TABLE - 1)], 0)
    ids = ids_land[...].reshape(SLOTS, EVENTS)
    mine = (ids >> 10) == me_t
    before = one_hot(row_of < col_of)
    rank = mm(one_hot(mine), before)
    turn = (iota((SLOTS, EVENTS), 0) & 7).astype(F32)
    picked = jnp.where(mine & (rank == turn), (ids & 1023).astype(F32) + 1.0, 0.0)
    asked = jnp.sum(picked, axis=1, keepdims=True) - 1.0
    loads[0].wait()
    hot = one_hot(iota((SLOTS, ROWS_T), 1) == asked.astype(I32))

    def stack_halves(values):
        cut = values.reshape(N_TABLE, CAP, WIDTH)
        return jnp.concatenate([cut[:, :, :256], cut[:, :, 256:]], axis=1).astype(BF16)

    fetch_send[...] = stack_halves(mm(hot, table_v[...]))
    to_table(fetch_send, fetch_land, 1, True)
    fetch_land[me_t] = fetch_send[me_t]

    tiles = []
    for q in range(4):
        piece = asked[64 * q : 64 * q + 64]
        twice = jnp.concatenate([piece, piece], axis=0)
        tiles.append(jnp.broadcast_to(twice, square).T[0:1])
    slots = jnp.concatenate(tiles + tiles, axis=0)
    slot_send[...] = slots
    slot_land[me_s] = slots
    to_seq(slot_send, slot_land, 2, False)

    place = iota((EVENTS, 2 * SLOTS), 1)
    pick_lo = one_hot(place == slot_col)
    pick_hi = one_hot(place == slot_col + CAP)
    loads[2].wait()
    wait_recv(fetch_land.at[pl.ds(0, N_TABLE - 1)], 1)
    fetched = fetch_land[...].reshape(2 * SLOTS, 256)
    emb = jnp.concatenate([mm(pick_lo, fetched), mm(pick_hi, fetched)], axis=1)

    center = emb - jnp.mean(emb, axis=1, keepdims=True)
    rs1 = lax.rsqrt(jnp.mean(center * center, axis=1, keepdims=True) + EPS)
    nx = center * rs1
    nx_s[...] = nx
    normed = nx.astype(BF16)

    def project(k):
        cols = slice(WIDTH * k, WIDTH * k + WIDTH)
        pre = mm(normed, w_in_v[:, cols])
        sigma = 0.5 + 0.5 * jnp.tanh(0.5 * pre)
        slope_s[:, cols] = sigma * (1.0 + pre * (1.0 - sigma))
        return (pre * sigma).astype(BF16).astype(F32)

    values, queries, keys = project(1), project(2) * 0.0625, project(3)
    lane_e = left((EVENTS, 128))
    lane_h = left((HEAD, 128))
    for p in range(4):
        cols = slice(128 * p, 128 * p + 128)
        kt, vt, qt = keys[:, cols], values[:, cols], queries[:, cols]
        q_lo, q_hi = qt[:64], qt[64:]
        qkv_send[2 * p, 0:128] = jnp.where(lane_e, kt, swap(vt)).astype(BF16)
        qkv_send[2 * p + 1, 0:128] = jnp.where(lane_e, swap(kt), vt).astype(BF16)
        qkv_send[2 * p, 128:192] = jnp.where(lane_h, q_lo, swap(q_hi)).astype(BF16)
        qkv_send[2 * p + 1, 128:192] = jnp.where(lane_h, swap(q_lo), q_hi).astype(BF16)
    to_heads(qkv_send, qkv_land, 3, True, qkv_sem)
    qkv_land[y] = qkv_send[y]

    gate = project(0)
    gate_t = gate.T
    u_t[...] = gate_t
    e_full = dz_t[...] * gate_t
    e_full = e_full - jnp.mean(e_full, axis=0, keepdims=True)
    e_send[...] = e_full.reshape(HEADS, HEAD, EVENTS).astype(BF16)
    to_heads(e_send, e_land, 4, True)
    e_land[y] = e_send[y]

    def pass_on(d, carry):
        peer = (y + HEADS - d) % HEADS

        @pl.when(d > 0)
        def _():
            pltpu.make_async_copy(qkv_land.at[peer], qkv_land.at[peer], qkv_sem.at[peer]).wait()

        remote(
            qkv_land.at[peer, pl.ds(0, 128)], kv_sib.at[peer], 5, {"seq": sibling}
        ).start()
        return carry

    lax.fori_loop(0, HEADS, pass_on, 0)

    for i in range(HEADS):
        block = qkv_land[i]
        kv_nat[pl.ds(pl.multiple_of((2 * i + core) * 64, 64), 64)] = block[0:64]
        kv_nat[pl.ds(pl.multiple_of((31 - 2 * i - core) * 64, 64), 64)] = block[64:128]
        packed = block[128:192].astype(F32)
        q_pad[64 * i : 64 * i + 64] = jnp.where(lane_h, packed, 0.0).astype(BF16)
        q_pad[64 * (15 - i) : 64 * (16 - i)] = jnp.where(lane_h, swap(packed), 0.0).astype(BF16)
    wait_recv(kv_sib, 5)
    for i in range(HEADS):
        block = kv_sib[i]
        kv_nat[pl.ds(pl.multiple_of((2 * i + 1 - core) * 64, 64), 64)] = block[0:64]
        kv_nat[pl.ds(pl.multiple_of((30 - 2 * i + core) * 64, 64), 64)] = block[64:128]
    for k in range(4):
        kv_t[k] = kv_nat[512 * k : 512 * k + 512].T

    def forward(t, carry):
        q = q_pad[pl.ds(pl.multiple_of(256 * t, 256), 256)]
        lane = 256 * t + iota((1, 256), 1)
        block_q = lane >> 6
        block_q = 2 * block_q + jnp.where(block_q < 8, core, 1 - core)
        pos_q = block_q * 64 + (lane & 63)

        def inner(k, total):
            index = t * (t + 1) // 2 + k
            kv = kv_nat[pl.ds(pl.multiple_of(512 * k, 512), 512)]
            h = mm_t(kv, q)
            pos_k = 512 * k + iota((512, 1), 0)
            h = jnp.where(pos_k <= pos_q, h, HIDDEN)
            th = jnp.tanh(h)
            a = (h + h * th).astype(BF16)
            a_t[index] = a
            g_t[index] = (1.0 + th) + h * (1.0 - th * th)
            return total + mm(kv_t[k, 64:128], a)

        total = lax.fori_loop(0, t + 1, inner, jnp.zeros((HEAD, 256), F32))
        y_t[2 * t] = total[:, :128]
        y_t[2 * t + 1] = total[:, 128:]
        return carry

    lax.fori_loop(0, 4, forward, 0)

    wait_recv(e_land.at[pl.ds(0, HEADS - 1)], 4)
    e_in = [e_land[i].astype(F32) for i in range(HEADS)]
    e_tiles = []
    for p in range(8):
        if p < 4:
            tile = jnp.where(lane_h, e_in[2 * p], swap(e_in[2 * p + 1]))
        else:
            tile = jnp.where(lane_h, swap(e_in[15 - 2 * p]), e_in[14 - 2 * p])
        e_tiles.append(tile[None])
    e_all = jnp.concatenate(e_tiles, axis=0)
    y_all = y_t[...]
    mean_h = jnp.sum(y_all, axis=1) * (1.0 / HEAD)
    spread = y_all - mean_h[:, None, :]
    stats = jnp.concatenate(
        [mean_h, jnp.sum(spread * spread, axis=1), jnp.sum(e_all * y_all, axis=1)], axis=0
    )
    stat_send[...] = stats
    stat_land[y] = stats
    to_heads(stat_send, stat_land, 6, False)

    wait_recv(slot_land.at[pl.ds(0, N_SEQ - 1)], 2)
    lane_8 = left((8, 128))

    def prepare(pair, carry):
        both = jnp.where(lane_8, slot_land[2 * pair], slot_land[2 * pair + 1]).astype(I32)
        span_rows = pl.ds(pl.multiple_of(128 * pair, 128), 128)
        for q in range(4):
            line = both[q : q + 1]
            hot_hi[q, pair] = one_hot(iota((256, 128), 0) == (line & 255))
            column = jnp.broadcast_to((line >> 8).astype(F32), square).T
            mask_lo[q, span_rows] = jnp.where(
                (col_of >> 5).astype(F32) == column, 1.0, 0.0
            )
        return carry

    lax.fori_loop(0, N_SEQ // 2, prepare, 0)

    wait_recv(stat_land.at[pl.ds(0, HEADS - 1)], 6)
    st = stat_land[...]
    means = st[:, 0:8]
    mean = jnp.sum(means, axis=0) * (1.0 / HEADS)
    off = means - mean[None]
    total = jnp.sum(st[:, 8:16], axis=0) + HEAD * jnp.sum(off * off, axis=0)
    rs2 = lax.rsqrt(total * (1.0 / WIDTH) + EPS)
    lean = rs2 * jnp.sum(st[:, 16:24], axis=0) * (1.0 / WIDTH)
    ny = (y_all - mean[:, None, :]) * rs2[:, None, :]
    dy = rs2[:, None, :] * (e_all - ny * lean[:, None, :])
    for p in range(8):
        tall = jnp.concatenate([jnp.zeros((HEAD, 128), F32), dy[p]], axis=0)
        dy_pad[128 * p : 128 * p + 128] = tall.T.astype(BF16)

    def by_source(tiles, i):
        if i % 2 == 0:
            return jnp.where(lane_h, tiles[i // 2], tiles[(15 - i) // 2])
        return swap(jnp.where(lane_h, tiles[(15 - i) // 2], tiles[i // 2]))

    for i in range(HEADS):
        ny_send[i] = by_source([ny[p] for p in range(8)], i).astype(BF16)
    to_heads(ny_send, ny_land, 7, True)
    ny_land[y] = ny_send[y]

    dq_t[...] = jnp.zeros_like(dq_t)

    def backward(k, carry):
        kv = kv_nat[pl.ds(pl.multiple_of(512 * k, 512), 512)]

        def inner(t, total):
            index = t * (t + 1) // 2 + k
            span_q = pl.ds(pl.multiple_of(256 * t, 256), 256)
            dy_q = dy_pad[span_q]
            ds = (mm_t(kv, dy_q) * g_t[index]).astype(BF16)
            dq_t[t] += mm(kv_t[k, 0:64], ds)
            return total + mm(ds, q_pad[span_q]) + mm(a_t[index], dy_q)

        total = lax.fori_loop(k, 4, inner, jnp.zeros((512, 128), F32))
        dkv_s[pl.ds(pl.multiple_of(512 * k, 512), 512)] = total
        return carry

    lax.fori_loop(0, 4, backward, 0)

    def both_halves(first, second):
        return jnp.concatenate(
            [
                dkv_s[pl.ds(pl.multiple_of(first * 64, 64), 64)],
                dkv_s[pl.ds(pl.multiple_of(second * 64, 64), 64)],
            ],
            axis=0,
        )

    for i in range(HEADS):
        sib_send[i] = both_halves(2 * i + 1 - core, 30 - 2 * i + core).astype(BF16)
    sibling_copy = remote(sib_send, sib_land, 8, {"seq": sibling})
    sibling_copy.start()

    dq_tiles = []
    for t in range(4):
        both = dq_t[t] * 0.0625
        dq_tiles += [both[:, :128], both[:, 128:]]
    for i in range(HEADS):
        back_send[i, 128:192] = by_source(dq_tiles, i).astype(BF16)
    wait_recv(sib_land, 8)
    for i in range(HEADS):
        own = both_halves(2 * i + core, 31 - 2 * i - core) + sib_land[i].astype(F32)
        back_send[i, 0:128] = own.astype(BF16)
    to_heads(back_send, back_land, 9, True)
    back_land[y] = back_send[y]

    wait_recv(ny_land.at[pl.ds(0, HEADS - 1)], 7)
    ny_full = ny_land[...].reshape(WIDTH, EVENTS).astype(F32)
    z_t = (ny_full * u_t[...]).astype(BF16)
    w_send[...] = mm(z_t, grad_s[...].astype(BF16)).reshape(N_TABLE, 16, WIDTH).astype(BF16)
    to_table(w_send, w_land, 10, True)
    w_land[me_t] = w_send[me_t]
    d_u = (dz_t[...] * ny_full).T

    wait_recv(back_land.at[pl.ds(0, HEADS - 1)], 9)
    d_k, d_v, d_q = [], [], []
    for p in range(4):
        first = back_land[2 * p, 0:128].astype(F32)
        second = back_land[2 * p + 1, 0:128].astype(F32)
        d_k.append(jnp.where(lane_e, first, swap(second)))
        d_v.append(jnp.where(lane_e, swap(first), second))
        pair = [back_land[2 * p + n, 128:192].astype(F32) for n in range(2)]
        d_q.append(jnp.concatenate(pair, axis=0).T)
    d_proj = jnp.concatenate([d_u] + d_v + d_q + d_k, axis=1)
    d_pre = (d_proj * slope_s[...]).astype(BF16)
    dn = mm_t(d_pre, w_in_v[...])
    nx = nx_s[...]
    first = jnp.mean(dn, axis=1, keepdims=True)
    second = jnp.mean(dn * nx, axis=1, keepdims=True)
    d_x = grad_s[...] + rs1 * (dn - first - nx * second)

    place_t = one_hot(iota((SLOTS, EVENTS), 0) == slot_row)
    dx_send[...] = stack_halves(mm(place_t, d_x.astype(BF16)))
    to_table(dx_send, dx_land, 11, True)
    dx_land[me_t] = dx_send[me_t]

    wait_recv(w_land.at[pl.ds(0, N_TABLE - 1)], 10)
    part = jnp.sum(w_land[...].astype(F32), axis=0).astype(BF16)
    part_send[...] = part
    part_land[me_s] = part
    to_seq(part_send, part_land, 12, False)

    wait_recv(dx_land.at[pl.ds(0, N_TABLE - 1)], 11)
    group = iota((64, 128), 1) >> 5
    for side in range(2):
        rows = dx_land[:, 8 * side : 8 * side + 8].astype(F32).reshape(SLOTS, 256)
        for tile in range(2):
            cut = rows[:, 128 * tile : 128 * tile + 128]
            turned = [cut] + [pltpu.roll(cut, 32 * r, 1) for r in range(1, 4)]
            for g in range(4):
                chunk = turned[(0 - g) % 4][0:64]
                for q in range(1, 4):
                    chunk = jnp.where(group == q, turned[(q - g) % 4][64 * q : 64 * q + 64], chunk)
                col_send[8 * side + 4 * tile + g] = chunk.astype(BF16)
    to_seq(col_send, col_land, 13, True)
    col_land[me_s] = col_send[me_s]

    wait_recv(part_land.at[pl.ds(0, N_SEQ - 1)], 12)
    w_grad_ref[...] = jnp.sum(part_land[...].astype(F32), axis=0)

    spread_of = iota((128, WIDTH), 1)
    spread_to = one_hot(
        iota((128, WIDTH), 0) == 32 * (spread_of >> 7) + (spread_of & 31)
    )
    wait_recv(col_land.at[pl.ds(0, N_SEQ - 1)], 13)
    wide = mm(col_land[...].reshape(N_SEQ * 64, 128), spread_to)
    total = jnp.zeros((256, 128), F32)
    for q in range(4):
        placed = (wide[:, 128 * q : 128 * q + 128] * mask_lo[q]).astype(BF16)
        hot_q = jnp.concatenate([hot_hi[q, pair] for pair in range(N_SEQ // 2)], axis=1)
        total = total + mm(hot_q, placed)
    out_ref[...] = total

    wait_sent(ids_land.at[pl.ds(0, N_TABLE - 1)], 0)
    wait_sent(fetch_send.at[pl.ds(0, N_TABLE - 1)], 1)
    wait_sent(slot_land.at[pl.ds(0, N_SEQ - 1)], 2)
    wait_sent(qkv_send.at[pl.ds(0, HEADS - 1)], 3)
    wait_sent(e_send.at[pl.ds(0, HEADS - 1)], 4)
    wait_sent(kv_sib, 5)
    wait_sent(stat_land.at[pl.ds(0, HEADS - 1)], 6)
    wait_sent(ny_send.at[pl.ds(0, HEADS - 1)], 7)
    wait_sent(sib_send, 8)
    wait_sent(back_send.at[pl.ds(0, HEADS - 1)], 9)
    wait_sent(w_send.at[pl.ds(0, N_TABLE - 1)], 10)
    wait_sent(dx_send.at[pl.ds(0, N_TABLE - 1)], 11)
    wait_sent(part_land.at[pl.ds(0, N_SEQ - 1)], 12)
    wait_sent(col_send.at[pl.ds(0, N_SEQ - 1)], 13)


def on_device(table, item_rows, lengths, w_in, w_out, cotangent):
    vmem = pl.BlockSpec(memory_space=pltpu.VMEM)
    smem = pl.BlockSpec(memory_space=pltpu.SMEM)
    anywhere = pl.BlockSpec(memory_space=pl.ANY)
    buf = pltpu.VMEM
    scratch = [
        buf((ROWS_T, WIDTH), BF16),
        buf((WIDTH, 4 * WIDTH), BF16),
        buf((WIDTH, WIDTH), BF16),
        buf((8, EVENTS), I32),
        buf((N_TABLE, 8, EVENTS), I32),
        buf((N_TABLE, 16, 256), BF16),
        buf((N_TABLE, 16, 256), BF16),
        buf((8, 128), F32),
        buf((N_SEQ, 8, 128), F32),
        buf((HEADS, 192, 128), BF16),
        buf((HEADS, 192, 128), BF16),
        buf((HEADS, 128, 128), BF16),
        buf((HEADS, HEAD, 128), BF16),
        buf((HEADS, HEAD, 128), BF16),
        buf((24, 128), F32),
        buf((HEADS, 24, 128), F32),
        buf((HEADS, HEAD, 128), BF16),
        buf((HEADS, HEAD, 128), BF16),
        buf((N_TABLE, 16, WIDTH), BF16),
        buf((N_TABLE, 16, WIDTH), BF16),
        buf((16, WIDTH), BF16),
        buf((N_SEQ, 16, WIDTH), BF16),
        buf((HEADS, 128, 128), BF16),
        buf((HEADS, 128, 128), BF16),
        buf((HEADS, 192, 128), BF16),
        buf((HEADS, 192, 128), BF16),
        buf((N_TABLE, 16, 256), BF16),
        buf((N_TABLE, 16, 256), BF16),
        buf((N_SEQ, 64, 128), BF16),
        buf((N_SEQ, 64, 128), BF16),
        buf((EVENTS, WIDTH), F32),
        buf((WIDTH, EVENTS), F32),
        buf((WIDTH, EVENTS), F32),
        buf((EVENTS, WIDTH), F32),
        buf((EVENTS, 4 * WIDTH), F32),
        buf((2048, 128), BF16),
        buf((4, 128, 512), BF16),
        buf((1024, 128), BF16),
        buf((1024, 128), BF16),
        buf((10, 512, 256), BF16),
        buf((10, 512, 256), F32),
        buf((8, HEAD, 128), F32),
        buf((4, HEAD, 256), F32),
        buf((2048, 128), F32),
        buf((4, N_SEQ // 2, 256, 128), BF16),
        buf((4, N_SEQ * 64, 128), F32),
        pltpu.SemaphoreType.DMA((3,)),
        pltpu.SemaphoreType.DMA((14,)),
        pltpu.SemaphoreType.DMA((14,)),
        pltpu.SemaphoreType.DMA((HEADS,)),
    ]
    sums, w_grad = pl.pallas_call(
        kernel,
        out_shape=(
            jax.ShapeDtypeStruct((256, 128), F32),
            jax.ShapeDtypeStruct((16, WIDTH), F32),
        ),
        in_specs=[vmem, smem, vmem, anywhere, anywhere, anywhere],
        out_specs=(vmem, vmem),
        scratch_shapes=scratch,
        compiler_params=pltpu.CompilerParams(
            collective_id=0, has_side_effects=True, vmem_limit_bytes=48 * 1024 * 1024
        ),
    )(item_rows, lengths, cotangent[0], table, w_in, w_out)
    table_grad = sums.reshape(256, 4, 32).transpose(1, 0, 2).reshape(ROWS_T, 32)
    return table_grad, w_grad


def solution(mesh):
    return jax.shard_map(
        on_device,
        mesh=mesh,
        in_specs=(
            P("table", None),
            P("table", "seq"),
            P("table"),
            P(),
            P(),
            P("table", "seq", None),
        ),
        out_specs=(P("table", "seq"), P("table", None)),
        check_vma=False,
    )
```

```python
import jax
import jax.numpy as jnp
from jax import lax
from jax.experimental import pallas as pl
from jax.experimental.pallas import tpu as pltpu
from jax.sharding import PartitionSpec as P

EPS = 1e-05
MESH = pl.DeviceIdType.MESH
F32 = jnp.float32
BF16 = jnp.bfloat16
I32 = jnp.int32

N_SEQ = 16
N_TABLE = 32
EVENTS = 128
WIDTH = 512
HEADS = 8
HEAD = 64
CAP = 8
ROWS_T = 1024
SLOTS = N_TABLE * CAP
HIDDEN = -64.0


def mm(a, b):
    return jnp.dot(a, b, preferred_element_type=F32)


def mm_t(a, b):
    return lax.dot_general(a, b, (((1,), (1,)), ((), ())), preferred_element_type=F32)


def iota(shape, dim):
    return lax.broadcasted_iota(I32, shape, dim)


def one_hot(mask):
    return jnp.where(mask, 1.0, 0.0).astype(BF16)


def swap(tile):
    return pltpu.roll(tile, 64, tile.ndim - 1)


def left(shape):
    return iota(shape, len(shape) - 1) < 64


def kernel(
    rows_hbm,
    len_ref,
    cot_hbm,
    table_hbm,
    w_in_hbm,
    w_out_hbm,
    out_ref,
    w_grad_ref,
    table_v,
    w_in_v,
    w_out_v,
    cot_v,
    rows_v,
    ids_land,
    fetch_send,
    fetch_land,
    slot_send,
    slot_land,
    kv_send,
    kv_own,
    q_send,
    q_land,
    kv_sib,
    e_send,
    e_land,
    stat_send,
    stat_land,
    ny_send,
    ny_land,
    w_send,
    w_land,
    part_send,
    part_land,
    sib_send,
    sib_land,
    dkv_send,
    dkv_land,
    dq_send,
    dq_land,
    dx_send,
    dx_land,
    col_send,
    col_land,
    grad_s,
    dz_t,
    u_t,
    nx_s,
    slope_s,
    kv_nat,
    kv_t,
    q_pad,
    dy_pad,
    a_t,
    g_t,
    y_t,
    dq_t,
    dkv_s,
    hot_hi,
    mask_lo,
    load_sem,
    send_sem,
    recv_sem,
    kv_sem,
    sib_sem,
):
    me_s = lax.axis_index("seq")
    me_t = lax.axis_index("table")
    y = me_s // 2
    core = me_s % 2
    sibling = me_s + 1 - 2 * core

    loads = [
        pltpu.make_async_copy(src, dst, load_sem.at[k])
        for k, (src, dst) in enumerate(
            (
                (rows_hbm, rows_v),
                (table_hbm, table_v),
                (cot_hbm, cot_v),
                (w_out_hbm, w_out_v),
                (w_in_hbm, w_in_v),
            )
        )
    ]
    for load in loads:
        load.start()

    barrier = pltpu.get_barrier_semaphore()

    def greet_table(d, carry):
        pl.semaphore_signal(
            barrier, inc=1, device_id={"table": (me_t + d) % N_TABLE}, device_id_type=MESH
        )
        return carry

    def greet_seq(d, carry):
        pl.semaphore_signal(
            barrier, inc=1, device_id={"seq": (me_s + d) % N_SEQ}, device_id_type=MESH
        )
        return carry

    lax.fori_loop(1, N_TABLE, greet_table, 0)
    lax.fori_loop(1, N_SEQ, greet_seq, 0)

    def remote(src, dst, k, where, recv=None):
        return pltpu.make_async_remote_copy(
            src_ref=src,
            dst_ref=dst,
            send_sem=send_sem.at[k],
            recv_sem=recv_sem.at[k] if recv is None else recv,
            device_id=where,
            device_id_type=MESH,
        )

    def far_first(n):
        return 4 + ((n + 1) // 2) * (2 * (n % 2) - 1)

    def to_table(src, dst, k, split):
        def body(d, carry):
            peer = (me_t + d) % N_TABLE
            remote(src.at[peer] if split else src, dst.at[me_t], k, {"table": peer}).start()
            return carry

        lax.fori_loop(1, N_TABLE, body, 0)

    def to_seq(src, dst, k, split):
        def body(d, carry):
            peer = 2 * ((y + far_first(d // 2)) % HEADS) + (core + 1 + d) % 2
            remote(src.at[peer] if split else src, dst.at[me_s], k, {"seq": peer}).start()
            return carry

        lax.fori_loop(0, N_SEQ - 1, body, 0)

    def to_heads(src, dst, k, split, sems=None):
        def body(d, carry):
            peer = (y + far_first(d)) % HEADS
            recv = None if sems is None else sems.at[y]
            remote(
                src.at[peer] if split else src, dst.at[y], k, {"seq": 2 * peer + core}, recv
            ).start()
            return carry

        lax.fori_loop(0, HEADS - 1, body, 0)

    def wait_recv(ref, k):
        pltpu.make_async_copy(ref, ref, recv_sem.at[k]).wait()

    def wait_sent(ref, k):
        pltpu.make_async_copy(ref, ref, send_sem.at[k]).wait()

    loads[0].wait()
    ids_row = rows_v[...]
    ids_land[me_t] = ids_row
    pl.semaphore_wait(barrier, N_TABLE - 1 + N_SEQ - 1)
    to_table(rows_v, ids_land, 0, False)

    square = (EVENTS, EVENTS)
    row_of, col_of = iota(square, 0), iota(square, 1)
    ids_wide = jnp.broadcast_to(ids_row, square)
    ids_col = jnp.sum(
        jnp.where(row_of == col_of, ids_wide.astype(F32), 0.0), axis=1, keepdims=True
    ).astype(I32)
    owner_row = ids_wide >> 10
    owner_col = jnp.broadcast_to(ids_col >> 10, square)
    same = owner_row == owner_col
    rank_col = jnp.sum(
        jnp.where(same & (col_of < row_of), 1.0, 0.0), axis=1, keepdims=True
    ).astype(I32)
    rank_row = jnp.sum(
        jnp.where(same & (row_of < col_of), 1.0, 0.0), axis=0, keepdims=True
    ).astype(I32)
    slot_col = (ids_col >> 10) * 16 + rank_col
    slot_row = (ids_row >> 10) * CAP + rank_row

    half = iota((EVENTS, 1), 0)
    span = jnp.where(half < 64, me_s, 2 * N_SEQ - 1 - me_s)
    live = (span * 64 + (half & 63)) < len_ref[0]
    loads[2].wait()
    grad = jnp.where(live, cot_v[...].astype(F32), 0.0)
    grad_b = grad.astype(BF16)
    grad_s[...] = grad
    loads[3].wait()
    dz_t[...] = mm_t(w_out_v[...], grad_b)

    wait_recv(ids_land.at[pl.ds(0, N_TABLE - 1)], 0)
    ids = jnp.broadcast_to(ids_land[...], (N_TABLE, CAP, EVENTS)).reshape(SLOTS, EVENTS)
    mine = (ids >> 10) == me_t
    before = one_hot(row_of < col_of)
    rank = mm(one_hot(mine), before)
    turn = (iota((SLOTS, EVENTS), 0) & 7).astype(F32)
    picked = jnp.where(mine & (rank == turn), (ids & 1023).astype(F32) + 1.0, 0.0)
    asked = jnp.sum(picked, axis=1, keepdims=True) - 1.0
    loads[1].wait()
    hot = one_hot(iota((SLOTS, ROWS_T), 1) == asked.astype(I32))

    def stack_halves(values):
        cut = values.reshape(N_TABLE, CAP, WIDTH)
        return jnp.concatenate([cut[:, :, :256], cut[:, :, 256:]], axis=1).astype(BF16)

    fetch_send[...] = stack_halves(mm(hot, table_v[...]))
    to_table(fetch_send, fetch_land, 1, True)
    fetch_land[me_t] = fetch_send[me_t]

    tiles = []
    for q in range(4):
        piece = asked[64 * q : 64 * q + 64]
        twice = jnp.concatenate([piece, piece], axis=0)
        tiles.append(jnp.broadcast_to(twice, square).T[0:1])
    slots = jnp.concatenate(tiles + tiles, axis=0)
    slot_send[...] = slots
    slot_land[me_s] = slots
    to_seq(slot_send, slot_land, 2, False)

    place = iota((EVENTS, 2 * SLOTS), 1)
    pick_lo = one_hot(place == slot_col)
    pick_hi = one_hot(place == slot_col + CAP)
    loads[4].wait()
    wait_recv(fetch_land.at[pl.ds(0, N_TABLE - 1)], 1)
    fetched = fetch_land[...].reshape(2 * SLOTS, 256)
    emb = jnp.concatenate([mm(pick_lo, fetched), mm(pick_hi, fetched)], axis=1)

    center = emb - jnp.mean(emb, axis=1, keepdims=True)
    rs1 = lax.rsqrt(jnp.mean(center * center, axis=1, keepdims=True) + EPS)
    nx = center * rs1
    nx_s[...] = nx
    normed = nx.astype(BF16)

    def project(k):
        cols = slice(WIDTH * k, WIDTH * k + WIDTH)
        pre = mm(normed, w_in_v[:, cols])
        sigma = 0.5 + 0.5 * jnp.tanh(0.5 * pre)
        slope_s[:, cols] = sigma * (1.0 + pre * (1.0 - sigma))
        return (pre * sigma).astype(BF16).astype(F32)

    lane_e = left((EVENTS, 128))
    lane_h = left((HEAD, 128))
    keys, values = project(3), project(1)
    for p in range(4):
        cols = slice(128 * p, 128 * p + 128)
        kt, vt = keys[:, cols], values[:, cols]
        kv_send[2 * p] = jnp.where(lane_e, kt, swap(vt)).astype(BF16)
        kv_send[2 * p + 1] = jnp.where(lane_e, swap(kt), vt).astype(BF16)
    to_heads(kv_send, kv_own, 3, True, kv_sem)
    kv_own[y] = kv_send[y]
    queries = project(2) * 0.0625
    for p in range(4):
        cols = slice(128 * p, 128 * p + 128)
        q_lo, q_hi = queries[:64, cols], queries[64:, cols]
        q_send[2 * p] = jnp.where(lane_h, q_lo, swap(q_hi)).astype(BF16)
        q_send[2 * p + 1] = jnp.where(lane_h, swap(q_lo), q_hi).astype(BF16)
    to_heads(q_send, q_land, 14, True)
    q_land[y] = q_send[y]
    gate = project(0)
    gate_t = gate.T
    u_t[...] = gate_t
    e_full = dz_t[...] * gate_t
    e_full = e_full - jnp.mean(e_full, axis=0, keepdims=True)
    e_send[...] = e_full.reshape(HEADS, HEAD, EVENTS).astype(BF16)
    to_heads(e_send, e_land, 4, True)
    e_land[y] = e_send[y]

    wait_recv(slot_land.at[pl.ds(0, N_SEQ - 1)], 2)
    lane_8 = left((8, 128))

    def prepare(pair, carry):
        both = jnp.where(lane_8, slot_land[2 * pair], slot_land[2 * pair + 1]).astype(I32)
        span_rows = pl.ds(pl.multiple_of(128 * pair, 128), 128)
        for q in range(4):
            line = both[q : q + 1]
            hot_hi[q, pair] = one_hot(iota((256, 128), 0) == (line & 255))
            column = jnp.broadcast_to((line >> 8).astype(F32), square).T
            mask_lo[q, span_rows] = jnp.where(
                (col_of >> 5).astype(F32) == column, 1.0, 0.0
            )
        return carry

    lax.fori_loop(0, N_SEQ // 2, prepare, 0)

    def pass_on(d, carry):
        peer = (y + far_first(7 - d)) % HEADS

        @pl.when(d > 0)
        def _():
            pltpu.make_async_copy(kv_own.at[peer], kv_own.at[peer], kv_sem.at[peer]).wait()

        remote(kv_own.at[peer], kv_sib.at[peer], 5, {"seq": sibling}).start()
        return carry

    lax.fori_loop(0, HEADS, pass_on, 0)

    for i in range(HEADS):
        block = kv_own[i]
        kv_nat[pl.ds(pl.multiple_of((2 * i + core) * 64, 64), 64)] = block[0:64]
        kv_nat[pl.ds(pl.multiple_of((31 - 2 * i - core) * 64, 64), 64)] = block[64:128]
    wait_recv(q_land.at[pl.ds(0, HEADS - 1)], 14)
    for i in range(HEADS):
        packed = q_land[i].astype(F32)
        q_pad[64 * i : 64 * i + 64] = jnp.where(lane_h, packed, 0.0).astype(BF16)
        q_pad[64 * (15 - i) : 64 * (16 - i)] = jnp.where(lane_h, swap(packed), 0.0).astype(BF16)
    wait_recv(kv_sib, 5)
    for i in range(HEADS):
        block = kv_sib[i]
        kv_nat[pl.ds(pl.multiple_of((2 * i + 1 - core) * 64, 64), 64)] = block[0:64]
        kv_nat[pl.ds(pl.multiple_of((30 - 2 * i + core) * 64, 64), 64)] = block[64:128]
    for k in range(4):
        kv_t[k] = kv_nat[512 * k : 512 * k + 512].T

    def forward(t, carry):
        q = q_pad[pl.ds(pl.multiple_of(256 * t, 256), 256)]
        lane = 256 * t + iota((1, 256), 1)
        block_q = lane >> 6
        block_q = 2 * block_q + jnp.where(block_q < 8, core, 1 - core)
        pos_q = block_q * 64 + (lane & 63)

        def inner(k, total):
            index = t * (t + 1) // 2 + k
            kv = kv_nat[pl.ds(pl.multiple_of(512 * k, 512), 512)]
            h = mm_t(kv, q)
            pos_k = 512 * k + iota((512, 1), 0)
            h = jnp.where(pos_k <= pos_q, h, HIDDEN)
            th = jnp.tanh(h)
            a = (h + h * th).astype(BF16)
            a_t[index] = a
            g_t[index] = h
            return total + mm(kv_t[k, 64:128], a)

        total = lax.fori_loop(0, t + 1, inner, jnp.zeros((HEAD, 256), F32))
        y_t[2 * t] = total[:, :128]
        y_t[2 * t + 1] = total[:, 128:]
        return carry

    lax.fori_loop(0, 4, forward, 0)

    wait_recv(e_land.at[pl.ds(0, HEADS - 1)], 4)
    e_in = [e_land[i].astype(F32) for i in range(HEADS)]
    e_tiles = []
    for p in range(8):
        if p < 4:
            tile = jnp.where(lane_h, e_in[2 * p], swap(e_in[2 * p + 1]))
        else:
            tile = jnp.where(lane_h, swap(e_in[15 - 2 * p]), e_in[14 - 2 * p])
        e_tiles.append(tile[None])
    e_all = jnp.concatenate(e_tiles, axis=0)
    y_all = y_t[...]
    mean_h = jnp.sum(y_all, axis=1) * (1.0 / HEAD)
    spread = y_all - mean_h[:, None, :]
    stats = jnp.concatenate(
        [mean_h, jnp.sum(spread * spread, axis=1), jnp.sum(e_all * y_all, axis=1)], axis=0
    )
    stat_send[...] = stats
    stat_land[y] = stats
    to_heads(stat_send, stat_land, 6, False)

    def slopes(index, carry):
        h = g_t[index]
        th = jnp.tanh(h)
        g_t[index] = (1.0 + th) + h * (1.0 - th * th)
        return carry

    lax.fori_loop(0, 10, slopes, 0)

    wait_recv(stat_land.at[pl.ds(0, HEADS - 1)], 6)
    st = stat_land[...]
    means = st[:, 0:8]
    mean = jnp.sum(means, axis=0) * (1.0 / HEADS)
    off = means - mean[None]
    total = jnp.sum(st[:, 8:16], axis=0) + HEAD * jnp.sum(off * off, axis=0)
    rs2 = lax.rsqrt(total * (1.0 / WIDTH) + EPS)
    lean = rs2 * jnp.sum(st[:, 16:24], axis=0) * (1.0 / WIDTH)
    ny = (y_all - mean[:, None, :]) * rs2[:, None, :]
    dy = rs2[:, None, :] * (e_all - ny * lean[:, None, :])
    for p in range(8):
        tall = jnp.concatenate([jnp.zeros((HEAD, 128), F32), dy[p]], axis=0)
        dy_pad[128 * p : 128 * p + 128] = tall.T.astype(BF16)

    def by_source(tiles, i):
        if i % 2 == 0:
            return jnp.where(lane_h, tiles[i // 2], tiles[(15 - i) // 2])
        return swap(jnp.where(lane_h, tiles[(15 - i) // 2], tiles[i // 2]))

    for i in range(HEADS):
        ny_send[i] = by_source([ny[p] for p in range(8)], i).astype(BF16)
    to_heads(ny_send, ny_land, 7, True)
    ny_land[y] = ny_send[y]

    dq_t[...] = jnp.zeros_like(dq_t)

    def backward(k, carry):
        kv = kv_nat[pl.ds(pl.multiple_of(512 * k, 512), 512)]

        def inner(t, total):
            index = t * (t + 1) // 2 + k
            span_q = pl.ds(pl.multiple_of(256 * t, 256), 256)
            dy_q = dy_pad[span_q]
            ds = (mm_t(kv, dy_q) * g_t[index]).astype(BF16)
            dq_t[t] += mm(kv_t[k, 0:64], ds)
            return total + mm(ds, q_pad[span_q]) + mm(a_t[index], dy_q)

        total = lax.fori_loop(k, 4, inner, jnp.zeros((512, 128), F32))
        dkv_s[pl.ds(pl.multiple_of(512 * k, 512), 512)] = total
        return carry

    def both_halves(first, second):
        return jnp.concatenate(
            [
                dkv_s[pl.ds(pl.multiple_of(first * 64, 64), 64)],
                dkv_s[pl.ds(pl.multiple_of(second * 64, 64), 64)],
            ],
            axis=0,
        )

    def to_sibling(part):
        for i in range(4 * part, 4 * part + 4):
            sib_send[i] = both_halves(2 * i + 1 - core, 30 - 2 * i + core).astype(BF16)
        span = pl.ds(4 * part, 4)
        remote(sib_send.at[span], sib_land.at[span], 8, {"seq": sibling}, sib_sem.at[part]).start()

    def to_sources(part):
        span = pl.ds(4 * part, 4)
        pltpu.make_async_copy(sib_land.at[span], sib_land.at[span], sib_sem.at[part]).wait()
        for i in range(4 * part, 4 * part + 4):
            own = both_halves(2 * i + core, 31 - 2 * i - core) + sib_land[i].astype(F32)
            dkv_send[i] = own.astype(BF16)

        def body(d, carry):
            peer = (y + far_first(d)) % HEADS

            @pl.when(peer // 4 == part)
            def _():
                remote(dkv_send.at[peer], dkv_land.at[y], 9, {"seq": 2 * peer + core}).start()

            return carry

        lax.fori_loop(0, HEADS - 1, body, 0)

    backward(1, 0)
    backward(2, 0)
    to_sibling(1)
    backward(3, 0)
    to_sources(1)
    backward(0, 0)
    to_sibling(0)
    dq_tiles = []
    for t in range(4):
        both = dq_t[t] * 0.0625
        dq_tiles += [both[:, :128], both[:, 128:]]
    for i in range(HEADS):
        dq_send[i] = by_source(dq_tiles, i).astype(BF16)
    to_heads(dq_send, dq_land, 13, True)
    dq_land[y] = dq_send[y]
    to_sources(0)
    dkv_land[y] = dkv_send[y]

    wait_recv(ny_land.at[pl.ds(0, HEADS - 1)], 7)
    ny_full = ny_land[...].reshape(WIDTH, EVENTS).astype(F32)
    z_t = (ny_full * u_t[...]).astype(BF16)
    w_send[...] = mm(z_t, grad_s[...].astype(BF16)).reshape(N_TABLE, 16, WIDTH).astype(BF16)
    to_table(w_send, w_land, 10, True)
    w_land[me_t] = w_send[me_t]
    d_u = (dz_t[...] * ny_full).T

    wait_recv(dkv_land.at[pl.ds(0, HEADS - 1)], 9)
    wait_recv(dq_land.at[pl.ds(0, HEADS - 1)], 13)
    d_k, d_v, d_q = [], [], []
    for p in range(4):
        first = dkv_land[2 * p].astype(F32)
        second = dkv_land[2 * p + 1].astype(F32)
        d_k.append(jnp.where(lane_e, first, swap(second)))
        d_v.append(jnp.where(lane_e, swap(first), second))
        pair = [dq_land[2 * p + n].astype(F32) for n in range(2)]
        d_q.append(jnp.concatenate(pair, axis=0).T)
    d_proj = jnp.concatenate([d_u] + d_v + d_q + d_k, axis=1)
    d_pre = (d_proj * slope_s[...]).astype(BF16)
    dn = mm_t(d_pre, w_in_v[...])
    nx = nx_s[...]
    first = jnp.mean(dn, axis=1, keepdims=True)
    second = jnp.mean(dn * nx, axis=1, keepdims=True)
    d_x = grad_s[...] + rs1 * (dn - first - nx * second)

    place_t = one_hot(iota((SLOTS, EVENTS), 0) == slot_row)
    dx_send[...] = stack_halves(mm(place_t, d_x.astype(BF16)))
    to_table(dx_send, dx_land, 11, True)
    dx_land[me_t] = dx_send[me_t]

    wait_recv(w_land.at[pl.ds(0, N_TABLE - 1)], 10)
    part = jnp.sum(w_land[...].astype(F32), axis=0).astype(BF16)
    part_send[...] = part
    part_land[me_s] = part
    to_seq(part_send, part_land, 12, False)

    wait_recv(dx_land.at[pl.ds(0, N_TABLE - 1)], 11)
    group = iota((64, 128), 1) >> 5
    for side in range(2):
        rows = dx_land[:, 8 * side : 8 * side + 8].astype(F32).reshape(SLOTS, 256)
        for tile in range(2):
            cut = rows[:, 128 * tile : 128 * tile + 128]
            turned = [cut] + [pltpu.roll(cut, 32 * r, 1) for r in range(1, 4)]
            for g in range(4):
                chunk = turned[(0 - g) % 4][0:64]
                for q in range(1, 4):
                    chunk = jnp.where(group == q, turned[(q - g) % 4][64 * q : 64 * q + 64], chunk)
                col_send[8 * side + 4 * tile + g] = chunk.astype(BF16)
    to_seq(col_send, col_land, 15, True)
    col_land[me_s] = col_send[me_s]

    wait_recv(part_land.at[pl.ds(0, N_SEQ - 1)], 12)
    w_grad_ref[...] = jnp.sum(part_land[...].astype(F32), axis=0)

    spread_of = iota((128, WIDTH), 1)
    spread_to = one_hot(
        iota((128, WIDTH), 0) == 32 * (spread_of >> 7) + (spread_of & 31)
    )
    wait_recv(col_land.at[pl.ds(0, N_SEQ - 1)], 15)
    wide = mm(col_land[...].reshape(N_SEQ * 64, 128), spread_to)
    total = jnp.zeros((256, 128), F32)
    for q in range(4):
        placed = (wide[:, 128 * q : 128 * q + 128] * mask_lo[q]).astype(BF16)
        hot_q = jnp.concatenate([hot_hi[q, pair] for pair in range(N_SEQ // 2)], axis=1)
        total = total + mm(hot_q, placed)
    turned = total.T
    for k in range(4):
        out_ref[:, 256 * k : 256 * k + 256] = turned[32 * k : 32 * k + 32]

    wait_sent(ids_land.at[pl.ds(0, N_TABLE - 1)], 0)
    wait_sent(fetch_send.at[pl.ds(0, N_TABLE - 1)], 1)
    wait_sent(slot_land.at[pl.ds(0, N_SEQ - 1)], 2)
    wait_sent(kv_send.at[pl.ds(0, HEADS - 1)], 3)
    wait_sent(q_send.at[pl.ds(0, HEADS - 1)], 14)
    wait_sent(e_send.at[pl.ds(0, HEADS - 1)], 4)
    wait_sent(kv_sib, 5)
    wait_sent(stat_land.at[pl.ds(0, HEADS - 1)], 6)
    wait_sent(ny_send.at[pl.ds(0, HEADS - 1)], 7)
    wait_sent(sib_send, 8)
    wait_sent(dkv_send.at[pl.ds(0, HEADS - 1)], 9)
    wait_sent(dq_send.at[pl.ds(0, HEADS - 1)], 13)
    wait_sent(w_send.at[pl.ds(0, N_TABLE - 1)], 10)
    wait_sent(dx_send.at[pl.ds(0, N_TABLE - 1)], 11)
    wait_sent(part_land.at[pl.ds(0, N_SEQ - 1)], 12)
    wait_sent(col_send.at[pl.ds(0, N_SEQ - 1)], 15)


def on_device(table, item_rows, lengths, w_in, w_out, cotangent):
    vmem = pl.BlockSpec(memory_space=pltpu.VMEM)
    smem = pl.BlockSpec(memory_space=pltpu.SMEM)
    anywhere = pl.BlockSpec(memory_space=pl.ANY)
    buf = pltpu.VMEM
    scratch = [
        buf((ROWS_T, WIDTH), BF16),
        buf((WIDTH, 4 * WIDTH), BF16),
        buf((WIDTH, WIDTH), BF16),
        buf((EVENTS, WIDTH), BF16),
        buf((1, EVENTS), I32),
        buf((N_TABLE, 1, EVENTS), I32),
        buf((N_TABLE, 16, 256), BF16),
        buf((N_TABLE, 16, 256), BF16),
        buf((8, 128), F32),
        buf((N_SEQ, 8, 128), F32),
        buf((HEADS, 128, 128), BF16),
        buf((HEADS, 128, 128), BF16),
        buf((HEADS, HEAD, 128), BF16),
        buf((HEADS, HEAD, 128), BF16),
        buf((HEADS, 128, 128), BF16),
        buf((HEADS, HEAD, 128), BF16),
        buf((HEADS, HEAD, 128), BF16),
        buf((24, 128), F32),
        buf((HEADS, 24, 128), F32),
        buf((HEADS, HEAD, 128), BF16),
        buf((HEADS, HEAD, 128), BF16),
        buf((N_TABLE, 16, WIDTH), BF16),
        buf((N_TABLE, 16, WIDTH), BF16),
        buf((16, WIDTH), BF16),
        buf((N_SEQ, 16, WIDTH), BF16),
        buf((HEADS, 128, 128), BF16),
        buf((HEADS, 128, 128), BF16),
        buf((HEADS, 128, 128), BF16),
        buf((HEADS, 128, 128), BF16),
        buf((HEADS, HEAD, 128), BF16),
        buf((HEADS, HEAD, 128), BF16),
        buf((N_TABLE, 16, 256), BF16),
        buf((N_TABLE, 16, 256), BF16),
        buf((N_SEQ, 64, 128), BF16),
        buf((N_SEQ, 64, 128), BF16),
        buf((EVENTS, WIDTH), F32),
        buf((WIDTH, EVENTS), F32),
        buf((WIDTH, EVENTS), F32),
        buf((EVENTS, WIDTH), F32),
        buf((EVENTS, 4 * WIDTH), F32),
        buf((2048, 128), BF16),
        buf((4, 128, 512), BF16),
        buf((1024, 128), BF16),
        buf((1024, 128), BF16),
        buf((10, 512, 256), BF16),
        buf((10, 512, 256), F32),
        buf((8, HEAD, 128), F32),
        buf((4, HEAD, 256), F32),
        buf((2048, 128), F32),
        buf((4, N_SEQ // 2, 256, 128), BF16),
        buf((4, N_SEQ * 64, 128), F32),
        pltpu.SemaphoreType.DMA((5,)),
        pltpu.SemaphoreType.DMA((16,)),
        pltpu.SemaphoreType.DMA((16,)),
        pltpu.SemaphoreType.DMA((HEADS,)),
        pltpu.SemaphoreType.DMA((2,)),
    ]
    sums, w_grad = pl.pallas_call(
        kernel,
        out_shape=(
            jax.ShapeDtypeStruct((32, ROWS_T), F32),
            jax.ShapeDtypeStruct((16, WIDTH), F32),
        ),
        in_specs=[anywhere, smem, anywhere, anywhere, anywhere, anywhere],
        out_specs=(vmem, vmem),
        scratch_shapes=scratch,
        compiler_params=pltpu.CompilerParams(
            collective_id=0, has_side_effects=True, vmem_limit_bytes=60 * 1024 * 1024
        ),
    )(item_rows, lengths, cotangent[0], table, w_in, w_out)
    return sums.T, w_grad


def solution(mesh):
    return jax.shard_map(
        on_device,
        mesh=mesh,
        in_specs=(
            P("table", None),
            P("table", "seq"),
            P("table"),
            P(),
            P(),
            P("table", "seq", None),
        ),
        out_specs=(P("table", "seq"), P("table", None)),
        check_vma=False,
    )
```

```python
import jax
import jax.numpy as jnp
from jax import lax
from jax.experimental import pallas as pl
from jax.experimental.pallas import tpu as pltpu
from jax.sharding import PartitionSpec as P

EPS = 1e-05
MESH = pl.DeviceIdType.MESH
F32 = jnp.float32
BF16 = jnp.bfloat16
I32 = jnp.int32

N_SEQ = 16
N_TABLE = 32
EVENTS = 128
WIDTH = 512
HEADS = 8
HEAD = 64
CAP = 8
ROWS_T = 1024
SLOTS = N_TABLE * CAP
HIDDEN = -64.0


def mm(a, b):
    return jnp.dot(a, b, preferred_element_type=F32)


def mm_t(a, b):
    return lax.dot_general(a, b, (((1,), (1,)), ((), ())), preferred_element_type=F32)


def iota(shape, dim):
    return lax.broadcasted_iota(I32, shape, dim)


def one_hot(mask):
    return jnp.where(mask, 1.0, 0.0).astype(BF16)


def swap(tile):
    return pltpu.roll(tile, 64, tile.ndim - 1)


def left(shape):
    return iota(shape, len(shape) - 1) < 64


def kernel(
    rows_hbm,
    len_ref,
    cot_hbm,
    table_hbm,
    w_in_hbm,
    w_out_hbm,
    out_ref,
    w_grad_ref,
    table_v,
    w_in_v,
    w_out_v,
    cot_v,
    rows_v,
    ids_land,
    fetch_send,
    fetch_land,
    slot_send,
    slot_land,
    kv_send,
    kv_own,
    q_send,
    q_land,
    kv_sib,
    e_send,
    e_land,
    stat_send,
    stat_land,
    ny_send,
    ny_land,
    w_send,
    w_land,
    part_send,
    part_land,
    sib_send,
    sib_land,
    dkv_send,
    dkv_land,
    dq_send,
    dq_land,
    dx_send,
    dx_land,
    col_send,
    col_land,
    grad_s,
    dz_t,
    u_t,
    nx_s,
    slope_s,
    kv_nat,
    kv_t,
    q_pad,
    dy_pad,
    a_t,
    g_t,
    y_t,
    dq_t,
    dkv_s,
    hot_hi,
    mask_lo,
    asked_s,
    load_sem,
    send_sem,
    recv_sem,
    kv_sem,
    sib_sem,
):
    me_s = lax.axis_index("seq")
    me_t = lax.axis_index("table")
    y = me_s // 2
    core = me_s % 2
    sibling = me_s + 1 - 2 * core

    loads = [
        pltpu.make_async_copy(src, dst, load_sem.at[k])
        for k, (src, dst) in enumerate(
            (
                (rows_hbm, rows_v),
                (table_hbm, table_v),
                (cot_hbm, cot_v),
                (w_out_hbm, w_out_v),
                (w_in_hbm, w_in_v),
            )
        )
    ]
    for load in loads:
        load.start()

    barrier = pltpu.get_barrier_semaphore()

    def greet_table(d, carry):
        pl.semaphore_signal(
            barrier, inc=1, device_id={"table": (me_t + d) % N_TABLE}, device_id_type=MESH
        )
        return carry

    def greet_seq(d, carry):
        pl.semaphore_signal(
            barrier, inc=1, device_id={"seq": (me_s + d) % N_SEQ}, device_id_type=MESH
        )
        return carry

    lax.fori_loop(1, N_TABLE, greet_table, 0)
    lax.fori_loop(1, N_SEQ, greet_seq, 0)

    def remote(src, dst, k, where, recv=None):
        return pltpu.make_async_remote_copy(
            src_ref=src,
            dst_ref=dst,
            send_sem=send_sem.at[k],
            recv_sem=recv_sem.at[k] if recv is None else recv,
            device_id=where,
            device_id_type=MESH,
        )

    def far_first(n):
        return 4 + ((n + 1) // 2) * (2 * (n % 2) - 1)

    def to_table(src, dst, k, split):
        def body(d, carry):
            peer = (me_t + d) % N_TABLE
            remote(src.at[peer] if split else src, dst.at[me_t], k, {"table": peer}).start()
            return carry

        lax.fori_loop(1, N_TABLE, body, 0)

    def to_table_group(src, dst, k, group):
        def body(d, carry):
            z = (me_t // 4 + far_first(d // 4)) % 8
            x = (me_t + 2 + ((d % 4 + 1) // 2) * (2 * (d % 2) - 1)) % 4
            peer = 4 * z + x
            remote(src.at[peer], dst.at[me_t], k, {"table": peer}).start()
            return carry

        lax.fori_loop(16 * group, 16 + 15 * group, body, 0)

    def to_seq(src, dst, k, split):
        def body(d, carry):
            peer = 2 * ((y + far_first(d // 2)) % HEADS) + (core + 1 + d) % 2
            remote(src.at[peer] if split else src, dst.at[me_s], k, {"seq": peer}).start()
            return carry

        lax.fori_loop(0, N_SEQ - 1, body, 0)

    def to_heads(src, dst, k, split, sems=None):
        def body(d, carry):
            peer = (y + far_first(d)) % HEADS
            recv = None if sems is None else sems.at[y]
            remote(
                src.at[peer] if split else src, dst.at[y], k, {"seq": 2 * peer + core}, recv
            ).start()
            return carry

        lax.fori_loop(0, HEADS - 1, body, 0)

    def wait_recv(ref, k):
        pltpu.make_async_copy(ref, ref, recv_sem.at[k]).wait()

    def wait_sent(ref, k):
        pltpu.make_async_copy(ref, ref, send_sem.at[k]).wait()

    def z_rows(n):
        return pl.multiple_of(32 * ((me_t // 4 + 6 + n) % 8), 32)

    loads[0].wait()
    ids_row = rows_v[...]
    ids_land[me_t] = ids_row
    pl.semaphore_wait(barrier, N_TABLE - 1 + N_SEQ - 1)
    to_table(rows_v, ids_land, 0, False)

    square = (EVENTS, EVENTS)
    row_of, col_of = iota(square, 0), iota(square, 1)
    ids_wide = jnp.broadcast_to(ids_row, square)
    ids_col = jnp.sum(
        jnp.where(row_of == col_of, ids_wide.astype(F32), 0.0), axis=1, keepdims=True
    ).astype(I32)
    owner_row = ids_wide >> 10
    owner_col = jnp.broadcast_to(ids_col >> 10, square)
    same = owner_row == owner_col
    rank_col = jnp.sum(
        jnp.where(same & (col_of < row_of), 1.0, 0.0), axis=1, keepdims=True
    ).astype(I32)
    rank_row = jnp.sum(
        jnp.where(same & (row_of < col_of), 1.0, 0.0), axis=0, keepdims=True
    ).astype(I32)
    slot_col = (ids_col >> 10) * 16 + rank_col
    slot_row = (ids_row >> 10) * CAP + rank_row

    half = iota((EVENTS, 1), 0)
    span = jnp.where(half < 64, me_s, 2 * N_SEQ - 1 - me_s)
    live = (span * 64 + (half & 63)) < len_ref[0]
    loads[2].wait()
    grad = jnp.where(live, cot_v[...].astype(F32), 0.0)
    grad_b = grad.astype(BF16)
    grad_s[...] = grad
    loads[3].wait()
    dz_t[...] = mm_t(w_out_v[...], grad_b)

    wait_recv(ids_land.at[pl.ds(0, N_TABLE - 1)], 0)
    ids = jnp.broadcast_to(ids_land[...], (N_TABLE, CAP, EVENTS)).reshape(SLOTS, EVENTS)
    mine = (ids >> 10) == me_t
    before = one_hot(row_of < col_of)
    rank = mm(one_hot(mine), before)
    turn = (iota((SLOTS, EVENTS), 0) & 7).astype(F32)
    picked = jnp.where(mine & (rank == turn), (ids & 1023).astype(F32) + 1.0, 0.0)
    asked = jnp.sum(picked, axis=1, keepdims=True) - 1.0
    loads[1].wait()
    hot = one_hot(iota((SLOTS, ROWS_T), 1) == asked.astype(I32))

    def stack_halves(values):
        cut = values.reshape(N_TABLE, CAP, WIDTH)
        return jnp.concatenate([cut[:, :, :256], cut[:, :, 256:]], axis=1).astype(BF16)

    fetch_send[...] = stack_halves(mm(hot, table_v[...]))
    to_table(fetch_send, fetch_land, 1, True)
    fetch_land[me_t] = fetch_send[me_t]

    asked_s[...] = jnp.broadcast_to(asked, (SLOTS, 128))
    tiles = []
    for n in range(8):
        piece = asked_s[pl.ds(z_rows(n), 32)]
        tiles.append(jnp.concatenate([piece] * 4, axis=0).T[0:1])
    slots = jnp.concatenate(tiles, axis=0)
    slot_send[...] = slots
    slot_land[me_s] = slots
    to_seq(slot_send, slot_land, 2, False)

    place = iota((EVENTS, 2 * SLOTS), 1)
    pick_lo = one_hot(place == slot_col)
    pick_hi = one_hot(place == slot_col + CAP)
    loads[4].wait()
    wait_recv(fetch_land.at[pl.ds(0, N_TABLE - 1)], 1)
    fetched = fetch_land[...].reshape(2 * SLOTS, 256)
    emb = jnp.concatenate([mm(pick_lo, fetched), mm(pick_hi, fetched)], axis=1)

    center = emb - jnp.mean(emb, axis=1, keepdims=True)
    rs1 = lax.rsqrt(jnp.mean(center * center, axis=1, keepdims=True) + EPS)
    nx = center * rs1
    nx_s[...] = nx
    normed = nx.astype(BF16)

    def project(k):
        cols = slice(WIDTH * k, WIDTH * k + WIDTH)
        pre = mm(normed, w_in_v[:, cols])
        sigma = 0.5 + 0.5 * jnp.tanh(0.5 * pre)
        slope_s[:, cols] = sigma * (1.0 + pre * (1.0 - sigma))
        return (pre * sigma).astype(BF16).astype(F32)

    lane_e = left((EVENTS, 128))
    lane_h = left((HEAD, 128))
    keys, values = project(3), project(1)
    for p in range(4):
        cols = slice(128 * p, 128 * p + 128)
        kt, vt = keys[:, cols], values[:, cols]
        kv_send[2 * p] = jnp.where(lane_e, kt, swap(vt)).astype(BF16)
        kv_send[2 * p + 1] = jnp.where(lane_e, swap(kt), vt).astype(BF16)
    to_heads(kv_send, kv_own, 3, True, kv_sem)
    kv_own[y] = kv_send[y]
    queries = project(2) * 0.0625
    for p in range(4):
        cols = slice(128 * p, 128 * p + 128)
        q_lo, q_hi = queries[:64, cols], queries[64:, cols]
        q_send[2 * p] = jnp.where(lane_h, q_lo, swap(q_hi)).astype(BF16)
        q_send[2 * p + 1] = jnp.where(lane_h, swap(q_lo), q_hi).astype(BF16)
    to_heads(q_send, q_land, 14, True)
    q_land[y] = q_send[y]
    gate = project(0)
    gate_t = gate.T
    u_t[...] = gate_t
    e_full = dz_t[...] * gate_t
    e_full = e_full - jnp.mean(e_full, axis=0, keepdims=True)
    e_send[...] = e_full.reshape(HEADS, HEAD, EVENTS).astype(BF16)
    to_heads(e_send, e_land, 4, True)
    e_land[y] = e_send[y]

    wait_recv(slot_land.at[pl.ds(0, N_SEQ - 1)], 2)
    part_8 = iota((8, 128), 1) >> 5

    def prepare(quad, carry):
        four = slot_land[4 * quad]
        for n in range(1, 4):
            four = jnp.where(part_8 == n, slot_land[4 * quad + n], four)
        four = four.astype(I32)
        span_rows = pl.ds(pl.multiple_of(128 * quad, 128), 128)
        for n in range(8):
            line = four[n : n + 1]
            hot_hi[n, quad] = one_hot(iota((256, 128), 0) == (line & 255))
            column = jnp.broadcast_to((line >> 8).astype(F32), square).T
            mask_lo[n, span_rows] = jnp.where((col_of >> 5).astype(F32) == column, 1.0, 0.0)
        return carry

    lax.fori_loop(0, N_SEQ // 4, prepare, 0)

    def pass_on(d, carry):
        peer = (y + far_first(7 - d)) % HEADS

        @pl.when(d > 0)
        def _():
            pltpu.make_async_copy(kv_own.at[peer], kv_own.at[peer], kv_sem.at[peer]).wait()

        remote(kv_own.at[peer], kv_sib.at[peer], 5, {"seq": sibling}).start()
        return carry

    lax.fori_loop(0, HEADS, pass_on, 0)

    for i in range(HEADS):
        block = kv_own[i]
        kv_nat[pl.ds(pl.multiple_of((2 * i + core) * 64, 64), 64)] = block[0:64]
        kv_nat[pl.ds(pl.multiple_of((31 - 2 * i - core) * 64, 64), 64)] = block[64:128]
    wait_recv(kv_sib, 5)
    for i in range(HEADS):
        block = kv_sib[i]
        kv_nat[pl.ds(pl.multiple_of((2 * i + 1 - core) * 64, 64), 64)] = block[0:64]
        kv_nat[pl.ds(pl.multiple_of((30 - 2 * i + core) * 64, 64), 64)] = block[64:128]
    for k in range(4):
        kv_t[k] = kv_nat[512 * k : 512 * k + 512].T
    wait_recv(q_land.at[pl.ds(0, HEADS - 1)], 14)
    for i in range(HEADS):
        packed = q_land[i].astype(F32)
        q_pad[64 * i : 64 * i + 64] = jnp.where(lane_h, packed, 0.0).astype(BF16)
        q_pad[64 * (15 - i) : 64 * (16 - i)] = jnp.where(lane_h, swap(packed), 0.0).astype(BF16)

    def forward(t, carry):
        q = q_pad[pl.ds(pl.multiple_of(256 * t, 256), 256)]
        lane = 256 * t + iota((1, 256), 1)
        block_q = lane >> 6
        block_q = 2 * block_q + jnp.where(block_q < 8, core, 1 - core)
        pos_q = block_q * 64 + (lane & 63)

        def inner(k, total):
            index = t * (t + 1) // 2 + k
            kv = kv_nat[pl.ds(pl.multiple_of(512 * k, 512), 512)]
            h = mm_t(kv, q)
            pos_k = 512 * k + iota((512, 1), 0)
            h = jnp.where(pos_k <= pos_q, h, HIDDEN)
            th = jnp.tanh(h)
            a = (h + h * th).astype(BF16)
            a_t[index] = a
            g_t[index] = h
            return total + mm(kv_t[k, 64:128], a)

        total = lax.fori_loop(0, t + 1, inner, jnp.zeros((HEAD, 256), F32))
        y_t[2 * t] = total[:, :128]
        y_t[2 * t + 1] = total[:, 128:]
        return carry

    lax.fori_loop(0, 4, forward, 0)

    wait_recv(e_land.at[pl.ds(0, HEADS - 1)], 4)
    e_in = [e_land[i].astype(F32) for i in range(HEADS)]
    e_tiles = []
    for p in range(8):
        if p < 4:
            tile = jnp.where(lane_h, e_in[2 * p], swap(e_in[2 * p + 1]))
        else:
            tile = jnp.where(lane_h, swap(e_in[15 - 2 * p]), e_in[14 - 2 * p])
        e_tiles.append(tile[None])
    e_all = jnp.concatenate(e_tiles, axis=0)
    y_all = y_t[...]
    mean_h = jnp.sum(y_all, axis=1) * (1.0 / HEAD)
    spread = y_all - mean_h[:, None, :]
    stats = jnp.concatenate(
        [mean_h, jnp.sum(spread * spread, axis=1), jnp.sum(e_all * y_all, axis=1)], axis=0
    )
    stat_send[...] = stats
    stat_land[y] = stats
    to_heads(stat_send, stat_land, 6, False)

    def slopes(index, carry):
        h = g_t[index]
        th = jnp.tanh(h)
        g_t[index] = (1.0 + th) + h * (1.0 - th * th)
        return carry

    lax.fori_loop(0, 10, slopes, 0)

    wait_recv(stat_land.at[pl.ds(0, HEADS - 1)], 6)
    st = stat_land[...]
    means = st[:, 0:8]
    mean = jnp.sum(means, axis=0) * (1.0 / HEADS)
    off = means - mean[None]
    total = jnp.sum(st[:, 8:16], axis=0) + HEAD * jnp.sum(off * off, axis=0)
    rs2 = lax.rsqrt(total * (1.0 / WIDTH) + EPS)
    lean = rs2 * jnp.sum(st[:, 16:24], axis=0) * (1.0 / WIDTH)
    ny = (y_all - mean[:, None, :]) * rs2[:, None, :]
    dy = rs2[:, None, :] * (e_all - ny * lean[:, None, :])
    for p in range(8):
        tall = jnp.concatenate([jnp.zeros((HEAD, 128), F32), dy[p]], axis=0)
        dy_pad[128 * p : 128 * p + 128] = tall.T.astype(BF16)

    def by_source(tiles, i):
        if i % 2 == 0:
            return jnp.where(lane_h, tiles[i // 2], tiles[(15 - i) // 2])
        return swap(jnp.where(lane_h, tiles[(15 - i) // 2], tiles[i // 2]))

    for i in range(HEADS):
        ny_send[i] = by_source([ny[p] for p in range(8)], i).astype(BF16)
    to_heads(ny_send, ny_land, 7, True)
    ny_land[y] = ny_send[y]

    dq_t[...] = jnp.zeros_like(dq_t)

    def backward(k, first, step, count, fresh):
        span_k = pl.ds(512 * k, 512)
        kv = kv_nat[span_k]

        def inner(n, total):
            t = first + step * n
            index = t * (t + 1) // 2 + k
            span_q = pl.ds(pl.multiple_of(256 * t, 256), 256)
            dy_q = dy_pad[span_q]
            ds = (mm_t(kv, dy_q) * g_t[index]).astype(BF16)
            dq_t[t] += mm(kv_t[k, 0:64], ds)
            return total + mm(ds, q_pad[span_q]) + mm(a_t[index], dy_q)

        start = jnp.zeros((512, 128), F32) if fresh else dkv_s[span_k]
        dkv_s[span_k] = lax.fori_loop(0, count, inner, start)

    def both_halves(first, second):
        return jnp.concatenate(
            [
                dkv_s[pl.ds(pl.multiple_of(first * 64, 64), 64)],
                dkv_s[pl.ds(pl.multiple_of(second * 64, 64), 64)],
            ],
            axis=0,
        )

    def to_sibling(part):
        for i in range(4 * part, 4 * part + 4):
            sib_send[i] = both_halves(2 * i + 1 - core, 30 - 2 * i + core).astype(BF16)
        span = pl.ds(4 * part, 4)
        remote(sib_send.at[span], sib_land.at[span], 8, {"seq": sibling}, sib_sem.at[part]).start()

    def to_sources(part):
        span = pl.ds(4 * part, 4)
        pltpu.make_async_copy(sib_land.at[span], sib_land.at[span], sib_sem.at[part]).wait()
        for i in range(4 * part, 4 * part + 4):
            own = both_halves(2 * i + core, 31 - 2 * i - core) + sib_land[i].astype(F32)
            dkv_send[i] = own.astype(BF16)

        some_heads(dkv_send, dkv_land, 9, part)

    def some_heads(src, dst, k, part):
        def body(d, carry):
            peer = (y + far_first(d)) % HEADS

            @pl.when(peer // 4 == part)
            def _():
                remote(src.at[peer], dst.at[y], k, {"seq": 2 * peer + core}).start()

            return carry

        lax.fori_loop(0, HEADS - 1, body, 0)

    def queries_back(part):
        dq_tiles = []
        for t in range(4):
            if (t in (1, 2)) == (part == 1):
                both = dq_t[t] * 0.0625
                dq_tiles += [both[:, :128], both[:, 128:]]
            else:
                dq_tiles += [None, None]
        for i in range(4 * part, 4 * part + 4):
            dq_send[i] = by_source(dq_tiles, i).astype(BF16)
        some_heads(dq_send, dq_land, 13, part)

    backward(1, 1, 1, 3, True)
    backward(2, 2, 1, 2, True)
    to_sibling(1)
    wait_recv(ny_land.at[pl.ds(0, HEADS - 1)], 7)
    ny_full = ny_land[...].reshape(WIDTH, EVENTS).astype(F32)
    z_t = (ny_full * u_t[...]).astype(BF16)
    w_send[...] = mm(z_t, grad_s[...].astype(BF16)).reshape(N_TABLE, 16, WIDTH).astype(BF16)
    to_table(w_send, w_land, 10, True)
    w_land[me_t] = w_send[me_t]
    d_u = (dz_t[...] * ny_full).T
    backward(0, 1, 1, 2, True)
    queries_back(1)
    to_sources(1)
    backward(0, 0, 3, 2, False)
    backward(3, 3, 1, 1, True)
    to_sibling(0)
    queries_back(0)
    to_sources(0)
    dq_land[y] = dq_send[y]
    dkv_land[y] = dkv_send[y]
    d_pre_u = (d_u * slope_s[:, 0:WIDTH]).astype(BF16)
    dn_u = mm_t(d_pre_u, w_in_v[:, 0:WIDTH])

    wait_recv(dkv_land.at[pl.ds(0, HEADS - 1)], 9)
    wait_recv(dq_land.at[pl.ds(0, HEADS - 1)], 13)
    d_k, d_v, d_q = [], [], []
    for p in range(4):
        first = dkv_land[2 * p].astype(F32)
        second = dkv_land[2 * p + 1].astype(F32)
        d_k.append(jnp.where(lane_e, first, swap(second)))
        d_v.append(jnp.where(lane_e, swap(first), second))
        pair = [dq_land[2 * p + n].astype(F32) for n in range(2)]
        d_q.append(jnp.concatenate(pair, axis=0).T)
    d_proj = jnp.concatenate(d_v + d_q + d_k, axis=1)
    d_pre = (d_proj * slope_s[:, WIDTH:]).astype(BF16)
    dn = dn_u + mm_t(d_pre, w_in_v[:, WIDTH:])
    nx = nx_s[...]
    first = jnp.mean(dn, axis=1, keepdims=True)
    second = jnp.mean(dn * nx, axis=1, keepdims=True)
    d_x = grad_s[...] + rs1 * (dn - first - nx * second)

    place_t = one_hot(iota((SLOTS, EVENTS), 0) == slot_row)
    dx_send[...] = stack_halves(mm(place_t, d_x.astype(BF16)))
    to_table_group(dx_send, dx_land, 11, 1)
    to_table_group(dx_send, dx_land, 16, 0)
    dx_land[me_t] = dx_send[me_t]

    wait_recv(w_land.at[pl.ds(0, N_TABLE - 1)], 10)
    part = jnp.sum(w_land[...].astype(F32), axis=0).astype(BF16)
    part_send[...] = part
    part_land[me_s] = part
    to_seq(part_send, part_land, 12, False)

    group = iota((32, 128), 1) >> 5
    spread_of = iota((128, WIDTH), 1)
    spread_to = one_hot(
        iota((128, WIDTH), 0) == 32 * (spread_of >> 7) + (spread_of & 31)
    )

    def columns(side):
        planes = [
            dx_land[pl.ds(pl.multiple_of(4 * ((me_t // 4 + 6 + n) % 8), 4), 4)].astype(F32)
            for n in range(4 * side, 4 * side + 4)
        ]
        for part in range(2):
            rows = [plane[:, 8 * part : 8 * part + 8].reshape(32, 256) for plane in planes]
            for tile in range(2):
                cuts = [row[:, 128 * tile : 128 * tile + 128] for row in rows]
                for g in range(4):
                    chunk = None
                    for q in range(4):
                        shift = 32 * ((q - g) % 4)
                        cut = pltpu.roll(cuts[q], shift, 1) if shift else cuts[q]
                        chunk = cut if q == 0 else jnp.where(group == q, cut, chunk)
                    col_send[side, 8 * part + 4 * tile + g] = chunk.astype(BF16)
        to_seq(col_send.at[side], col_land.at[side], 15 if side == 0 else 17, True)
        col_land[side, me_s] = col_send[side, me_s]

    def placed(side, total):
        wide = mm(col_land[side].reshape(N_SEQ * 32, 128), spread_to)
        for q in range(4):
            n = 4 * side + q
            put = (wide[:, 128 * q : 128 * q + 128] * mask_lo[n]).astype(BF16)
            hot_q = jnp.concatenate([hot_hi[n, quad] for quad in range(N_SEQ // 4)], axis=1)
            total = total + mm(hot_q, put)
        return total

    wait_recv(dx_land.at[pl.ds(0, 15)], 11)
    columns(0)
    wait_recv(dx_land.at[pl.ds(0, 16)], 16)
    columns(1)

    wait_recv(part_land.at[pl.ds(0, N_SEQ - 1)], 12)
    w_grad_ref[...] = jnp.sum(part_land[...].astype(F32), axis=0)

    wait_recv(col_land.at[0, pl.ds(0, N_SEQ - 1)], 15)
    total = placed(0, jnp.zeros((256, 128), F32))
    wait_recv(col_land.at[1, pl.ds(0, N_SEQ - 1)], 17)
    total = placed(1, total)
    turned = total.T
    for k in range(4):
        out_ref[:, 256 * k : 256 * k + 256] = turned[32 * k : 32 * k + 32]

    wait_sent(ids_land.at[pl.ds(0, N_TABLE - 1)], 0)
    wait_sent(fetch_send.at[pl.ds(0, N_TABLE - 1)], 1)
    wait_sent(slot_land.at[pl.ds(0, N_SEQ - 1)], 2)
    wait_sent(kv_send.at[pl.ds(0, HEADS - 1)], 3)
    wait_sent(q_send.at[pl.ds(0, HEADS - 1)], 14)
    wait_sent(e_send.at[pl.ds(0, HEADS - 1)], 4)
    wait_sent(kv_sib, 5)
    wait_sent(stat_land.at[pl.ds(0, HEADS - 1)], 6)
    wait_sent(ny_send.at[pl.ds(0, HEADS - 1)], 7)
    wait_sent(sib_send, 8)
    wait_sent(dkv_send.at[pl.ds(0, HEADS - 1)], 9)
    wait_sent(dq_send.at[pl.ds(0, HEADS - 1)], 13)
    wait_sent(w_send.at[pl.ds(0, N_TABLE - 1)], 10)
    wait_sent(dx_send.at[pl.ds(0, 15)], 11)
    wait_sent(dx_send.at[pl.ds(0, 16)], 16)
    wait_sent(part_land.at[pl.ds(0, N_SEQ - 1)], 12)
    wait_sent(col_send.at[0, pl.ds(0, N_SEQ - 1)], 15)
    wait_sent(col_send.at[1, pl.ds(0, N_SEQ - 1)], 17)


def on_device(table, item_rows, lengths, w_in, w_out, cotangent):
    vmem = pl.BlockSpec(memory_space=pltpu.VMEM)
    smem = pl.BlockSpec(memory_space=pltpu.SMEM)
    anywhere = pl.BlockSpec(memory_space=pl.ANY)
    buf = pltpu.VMEM
    scratch = [
        buf((ROWS_T, WIDTH), BF16),
        buf((WIDTH, 4 * WIDTH), BF16),
        buf((WIDTH, WIDTH), BF16),
        buf((EVENTS, WIDTH), BF16),
        buf((1, EVENTS), I32),
        buf((N_TABLE, 1, EVENTS), I32),
        buf((N_TABLE, 16, 256), BF16),
        buf((N_TABLE, 16, 256), BF16),
        buf((8, 128), F32),
        buf((N_SEQ, 8, 128), F32),
        buf((HEADS, 128, 128), BF16),
        buf((HEADS, 128, 128), BF16),
        buf((HEADS, HEAD, 128), BF16),
        buf((HEADS, HEAD, 128), BF16),
        buf((HEADS, 128, 128), BF16),
        buf((HEADS, HEAD, 128), BF16),
        buf((HEADS, HEAD, 128), BF16),
        buf((24, 128), F32),
        buf((HEADS, 24, 128), F32),
        buf((HEADS, HEAD, 128), BF16),
        buf((HEADS, HEAD, 128), BF16),
        buf((N_TABLE, 16, WIDTH), BF16),
        buf((N_TABLE, 16, WIDTH), BF16),
        buf((16, WIDTH), BF16),
        buf((N_SEQ, 16, WIDTH), BF16),
        buf((HEADS, 128, 128), BF16),
        buf((HEADS, 128, 128), BF16),
        buf((HEADS, 128, 128), BF16),
        buf((HEADS, 128, 128), BF16),
        buf((HEADS, HEAD, 128), BF16),
        buf((HEADS, HEAD, 128), BF16),
        buf((N_TABLE, 16, 256), BF16),
        buf((N_TABLE, 16, 256), BF16),
        buf((2, N_SEQ, 32, 128), BF16),
        buf((2, N_SEQ, 32, 128), BF16),
        buf((EVENTS, WIDTH), F32),
        buf((WIDTH, EVENTS), F32),
        buf((WIDTH, EVENTS), F32),
        buf((EVENTS, WIDTH), F32),
        buf((EVENTS, 4 * WIDTH), F32),
        buf((2048, 128), BF16),
        buf((4, 128, 512), BF16),
        buf((1024, 128), BF16),
        buf((1024, 128), BF16),
        buf((10, 512, 256), BF16),
        buf((10, 512, 256), F32),
        buf((8, HEAD, 128), F32),
        buf((4, HEAD, 256), F32),
        buf((2048, 128), F32),
        buf((8, N_SEQ // 4, 256, 128), BF16),
        buf((8, N_SEQ * 32, 128), F32),
        buf((SLOTS, 128), F32),
        pltpu.SemaphoreType.DMA((5,)),
        pltpu.SemaphoreType.DMA((18,)),
        pltpu.SemaphoreType.DMA((18,)),
        pltpu.SemaphoreType.DMA((HEADS,)),
        pltpu.SemaphoreType.DMA((2,)),
    ]
    sums, w_grad = pl.pallas_call(
        kernel,
        out_shape=(
            pltpu.VMEM((32, ROWS_T), F32),
            pltpu.VMEM((16, WIDTH), F32),
        ),
        in_specs=[anywhere, smem, anywhere, anywhere, anywhere, anywhere],
        out_specs=(vmem, vmem),
        scratch_shapes=scratch,
        compiler_params=pltpu.CompilerParams(
            collective_id=0, has_side_effects=True, vmem_limit_bytes=56 * 1024 * 1024
        ),
    )(item_rows, lengths, cotangent[0], table, w_in, w_out)
    return sums.T, w_grad


def solution(mesh):
    return jax.shard_map(
        on_device,
        mesh=mesh,
        in_specs=(
            P("table", None),
            P("table", "seq"),
            P("table"),
            P(),
            P(),
            P("table", "seq", None),
        ),
        out_specs=(P("table", "seq"), P("table", None)),
        check_vma=False,
    )
```

```python
import jax
import jax.numpy as jnp
from jax import lax
from jax.experimental import pallas as pl
from jax.experimental.pallas import tpu as pltpu
from jax.sharding import PartitionSpec as P

EPS = 1e-05
MESH = pl.DeviceIdType.MESH
F32 = jnp.float32
BF16 = jnp.bfloat16
I32 = jnp.int32

N_SEQ = 16
N_TABLE = 32
EVENTS = 128
WIDTH = 512
HEADS = 8
HEAD = 64
CAP = 8
ROWS_T = 1024
SLOTS = N_TABLE * CAP
HIDDEN = -64.0


def mm(a, b):
    return jnp.dot(a, b, preferred_element_type=F32)


def mm_t(a, b):
    return lax.dot_general(a, b, (((1,), (1,)), ((), ())), preferred_element_type=F32)


def iota(shape, dim):
    return lax.broadcasted_iota(I32, shape, dim)


def one_hot(mask):
    return jnp.where(mask, 1.0, 0.0).astype(BF16)


def swap(tile):
    return pltpu.roll(tile, 64, tile.ndim - 1)


def left(shape):
    return iota(shape, len(shape) - 1) < 64


def kernel(
    rows_hbm,
    len_ref,
    cot_hbm,
    table_hbm,
    w_in_hbm,
    w_out_hbm,
    out_ref,
    w_grad_ref,
    table_v,
    w_in_v,
    w_out_v,
    cot_v,
    rows_v,
    ids_land,
    fetch_send,
    fetch_land,
    slot_send,
    slot_land,
    kv_send,
    kv_own,
    q_send,
    q_land,
    kv_sib,
    e_send,
    e_land,
    stat_send,
    stat_land,
    ny_send,
    ny_land,
    w_term,
    w_sib_send,
    w_sib_land,
    w_send,
    w_land,
    part_send,
    part_land,
    sib_send,
    sib_land,
    dkv_send,
    dkv_land,
    dq_send,
    dq_land,
    dx_send,
    dx_land,
    col_send,
    col_land,
    grad_s,
    dz_t,
    u_t,
    nx_s,
    slope_s,
    kv_nat,
    kv_t,
    q_pad,
    dy_pad,
    a_t,
    g_t,
    y_t,
    dq_t,
    dkv_s,
    hot_hi,
    mask_lo,
    asked_s,
    load_sem,
    send_sem,
    recv_sem,
    kv_sem,
    sib_sem,
):
    me_s = lax.axis_index("seq")
    me_t = lax.axis_index("table")
    y = me_s // 2
    core = me_s % 2
    sibling = me_s + 1 - 2 * core
    owns_w = core == me_t // 16

    loads = [
        pltpu.make_async_copy(src, dst, load_sem.at[k])
        for k, (src, dst) in enumerate(
            (
                (rows_hbm, rows_v),
                (table_hbm, table_v),
                (cot_hbm, cot_v),
                (w_out_hbm, w_out_v),
                (w_in_hbm, w_in_v),
            )
        )
    ]
    for load in loads:
        load.start()

    barrier = pltpu.get_barrier_semaphore()

    def greet_table(d, carry):
        pl.semaphore_signal(
            barrier, inc=1, device_id={"table": (me_t + d) % N_TABLE}, device_id_type=MESH
        )
        return carry

    def greet_seq(d, carry):
        pl.semaphore_signal(
            barrier, inc=1, device_id={"seq": (me_s + d) % N_SEQ}, device_id_type=MESH
        )
        return carry

    lax.fori_loop(1, N_TABLE, greet_table, 0)
    lax.fori_loop(1, N_SEQ, greet_seq, 0)

    def remote(src, dst, k, where, recv=None):
        return pltpu.make_async_remote_copy(
            src_ref=src,
            dst_ref=dst,
            send_sem=send_sem.at[k],
            recv_sem=recv_sem.at[k] if recv is None else recv,
            device_id=where,
            device_id_type=MESH,
        )

    def far_first(n):
        return 4 + ((n + 1) // 2) * (2 * (n % 2) - 1)

    def to_table(src, dst, k, split):
        def body(d, carry):
            peer = (me_t + d) % N_TABLE
            remote(src.at[peer] if split else src, dst.at[me_t], k, {"table": peer}).start()
            return carry

        lax.fori_loop(1, N_TABLE, body, 0)

    def to_table_group(src, dst, k, group):
        def body(d, carry):
            z = (me_t // 4 + far_first(d // 4)) % 8
            x = (me_t + 2 + ((d % 4 + 1) // 2) * (2 * (d % 2) - 1)) % 4
            peer = 4 * z + x
            remote(src.at[peer], dst.at[me_t], k, {"table": peer}).start()
            return carry

        lax.fori_loop(16 * group, 16 + 15 * group, body, 0)

    def to_seq(src, dst, k, split):
        def body(d, carry):
            peer = 2 * ((y + far_first(d // 2)) % HEADS) + (core + 1 + d) % 2
            remote(src.at[peer] if split else src, dst.at[me_s], k, {"seq": peer}).start()
            return carry

        lax.fori_loop(0, N_SEQ - 1, body, 0)

    def to_heads(src, dst, k, split, sems=None):
        def body(d, carry):
            peer = (y + far_first(d)) % HEADS
            recv = None if sems is None else sems.at[y]
            remote(
                src.at[peer] if split else src, dst.at[y], k, {"seq": 2 * peer + core}, recv
            ).start()
            return carry

        lax.fori_loop(0, HEADS - 1, body, 0)

    def wait_recv(ref, k):
        pltpu.make_async_copy(ref, ref, recv_sem.at[k]).wait()

    def wait_sent(ref, k):
        pltpu.make_async_copy(ref, ref, send_sem.at[k]).wait()

    def z_rows(n):
        return pl.multiple_of(32 * ((me_t // 4 + 6 + n) % 8), 32)

    loads[0].wait()
    ids_row = rows_v[...]
    ids_land[me_t] = ids_row
    pl.semaphore_wait(barrier, N_TABLE - 1 + N_SEQ - 1)
    to_table(rows_v, ids_land, 0, False)

    square = (EVENTS, EVENTS)
    row_of, col_of = iota(square, 0), iota(square, 1)
    ids_wide = jnp.broadcast_to(ids_row, square)
    ids_col = jnp.sum(
        jnp.where(row_of == col_of, ids_wide.astype(F32), 0.0), axis=1, keepdims=True
    ).astype(I32)
    owner_row = ids_wide >> 10
    owner_col = jnp.broadcast_to(ids_col >> 10, square)
    same = owner_row == owner_col
    rank_col = jnp.sum(
        jnp.where(same & (col_of < row_of), 1.0, 0.0), axis=1, keepdims=True
    ).astype(I32)
    rank_row = jnp.sum(
        jnp.where(same & (row_of < col_of), 1.0, 0.0), axis=0, keepdims=True
    ).astype(I32)
    slot_col = (ids_col >> 10) * 16 + rank_col
    slot_row = (ids_row >> 10) * CAP + rank_row

    half = iota((EVENTS, 1), 0)
    span = jnp.where(half < 64, me_s, 2 * N_SEQ - 1 - me_s)
    live = (span * 64 + (half & 63)) < len_ref[0]
    loads[2].wait()
    grad = jnp.where(live, cot_v[...].astype(F32), 0.0)
    grad_b = grad.astype(BF16)
    grad_s[...] = grad
    loads[3].wait()
    dz_t[...] = mm_t(w_out_v[...], grad_b)

    wait_recv(ids_land.at[pl.ds(0, N_TABLE - 1)], 0)
    ids = jnp.broadcast_to(ids_land[...], (N_TABLE, CAP, EVENTS)).reshape(SLOTS, EVENTS)
    mine = (ids >> 10) == me_t
    before = one_hot(row_of < col_of)
    rank = mm(one_hot(mine), before)
    turn = (iota((SLOTS, EVENTS), 0) & 7).astype(F32)
    picked = jnp.where(mine & (rank == turn), (ids & 1023).astype(F32) + 1.0, 0.0)
    asked = jnp.sum(picked, axis=1, keepdims=True) - 1.0
    loads[1].wait()
    hot = one_hot(iota((SLOTS, ROWS_T), 1) == asked.astype(I32))

    def stack_halves(values):
        cut = values.reshape(N_TABLE, CAP, WIDTH)
        return jnp.concatenate([cut[:, :, :256], cut[:, :, 256:]], axis=1).astype(BF16)

    fetch_send[...] = stack_halves(mm(hot, table_v[...]))
    to_table(fetch_send, fetch_land, 1, True)
    fetch_land[me_t] = fetch_send[me_t]

    asked_s[...] = jnp.broadcast_to(asked, (SLOTS, 128))
    tiles = []
    for n in range(8):
        piece = asked_s[pl.ds(z_rows(n), 32)]
        tiles.append(jnp.concatenate([piece] * 4, axis=0).T[0:1])
    slots = jnp.concatenate(tiles, axis=0)
    slot_send[...] = slots
    slot_land[me_s] = slots
    to_seq(slot_send, slot_land, 2, False)

    place = iota((EVENTS, 2 * SLOTS), 1)
    pick_lo = one_hot(place == slot_col)
    pick_hi = one_hot(place == slot_col + CAP)
    loads[4].wait()
    wait_recv(fetch_land.at[pl.ds(0, N_TABLE - 1)], 1)
    fetched = fetch_land[...].reshape(2 * SLOTS, 256)
    emb = jnp.concatenate([mm(pick_lo, fetched), mm(pick_hi, fetched)], axis=1)

    center = emb - jnp.mean(emb, axis=1, keepdims=True)
    rs1 = lax.rsqrt(jnp.mean(center * center, axis=1, keepdims=True) + EPS)
    nx = center * rs1
    nx_s[...] = nx
    normed = nx.astype(BF16)

    def project(k):
        cols = slice(WIDTH * k, WIDTH * k + WIDTH)
        pre = mm(normed, w_in_v[:, cols])
        sigma = 0.5 + 0.5 * jnp.tanh(0.5 * pre)
        slope_s[:, cols] = sigma * (1.0 + pre * (1.0 - sigma))
        return (pre * sigma).astype(BF16).astype(F32)

    lane_e = left((EVENTS, 128))
    lane_h = left((HEAD, 128))
    keys, values = project(3), project(1)
    for p in range(4):
        cols = slice(128 * p, 128 * p + 128)
        kt, vt = keys[:, cols], values[:, cols]
        kv_send[2 * p] = jnp.where(lane_e, kt, swap(vt)).astype(BF16)
        kv_send[2 * p + 1] = jnp.where(lane_e, swap(kt), vt).astype(BF16)
    to_heads(kv_send, kv_own, 3, True, kv_sem)
    kv_own[y] = kv_send[y]
    queries = project(2) * 0.0625
    for p in range(4):
        cols = slice(128 * p, 128 * p + 128)
        q_lo, q_hi = queries[:64, cols], queries[64:, cols]
        q_send[2 * p] = jnp.where(lane_h, q_lo, swap(q_hi)).astype(BF16)
        q_send[2 * p + 1] = jnp.where(lane_h, swap(q_lo), q_hi).astype(BF16)
    to_heads(q_send, q_land, 14, True)
    q_land[y] = q_send[y]
    gate = project(0)
    gate_t = gate.T
    u_t[...] = gate_t
    e_full = dz_t[...] * gate_t
    e_full = e_full - jnp.mean(e_full, axis=0, keepdims=True)
    e_send[...] = e_full.reshape(HEADS, HEAD, EVENTS).astype(BF16)
    to_heads(e_send, e_land, 4, True)
    e_land[y] = e_send[y]

    wait_recv(slot_land.at[pl.ds(0, N_SEQ - 1)], 2)
    part_8 = iota((8, 128), 1) >> 5

    def prepare(quad, carry):
        four = slot_land[4 * quad]
        for n in range(1, 4):
            four = jnp.where(part_8 == n, slot_land[4 * quad + n], four)
        four = four.astype(I32)
        span_rows = pl.ds(pl.multiple_of(128 * quad, 128), 128)
        for n in range(8):
            line = four[n : n + 1]
            hot_hi[n, quad] = one_hot(iota((256, 128), 0) == (line & 255))
            column = jnp.broadcast_to((line >> 8).astype(F32), square).T
            mask_lo[n, span_rows] = jnp.where((col_of >> 5).astype(F32) == column, 1.0, 0.0)
        return carry

    lax.fori_loop(0, N_SEQ // 4, prepare, 0)

    def pass_on(d, carry):
        peer = (y + jnp.where(d == 0, 0, far_first(d - 1))) % HEADS

        @pl.when(d > 0)
        def _():
            pltpu.make_async_copy(kv_own.at[peer], kv_own.at[peer], kv_sem.at[peer]).wait()

        remote(kv_own.at[peer], kv_sib.at[peer], 5, {"seq": sibling}).start()
        return carry

    lax.fori_loop(0, HEADS, pass_on, 0)

    for i in range(HEADS):
        block = kv_own[i]
        kv_nat[pl.ds(pl.multiple_of((2 * i + core) * 64, 64), 64)] = block[0:64]
        kv_nat[pl.ds(pl.multiple_of((31 - 2 * i - core) * 64, 64), 64)] = block[64:128]
    wait_recv(kv_sib, 5)
    for i in range(HEADS):
        block = kv_sib[i]
        kv_nat[pl.ds(pl.multiple_of((2 * i + 1 - core) * 64, 64), 64)] = block[0:64]
        kv_nat[pl.ds(pl.multiple_of((30 - 2 * i + core) * 64, 64), 64)] = block[64:128]
    for k in range(4):
        kv_t[k] = kv_nat[512 * k : 512 * k + 512].T
    wait_recv(q_land.at[pl.ds(0, HEADS - 1)], 14)
    for i in range(HEADS):
        packed = q_land[i].astype(F32)
        q_pad[64 * i : 64 * i + 64] = jnp.where(lane_h, packed, 0.0).astype(BF16)
        q_pad[64 * (15 - i) : 64 * (16 - i)] = jnp.where(lane_h, swap(packed), 0.0).astype(BF16)

    def forward(t, carry):
        q = q_pad[pl.ds(pl.multiple_of(256 * t, 256), 256)]
        lane = 256 * t + iota((1, 256), 1)
        block_q = lane >> 6
        block_q = 2 * block_q + jnp.where(block_q < 8, core, 1 - core)
        pos_q = block_q * 64 + (lane & 63)

        def inner(k, total):
            index = t * (t + 1) // 2 + k
            kv = kv_nat[pl.ds(pl.multiple_of(512 * k, 512), 512)]
            h = mm_t(kv, q)
            pos_k = 512 * k + iota((512, 1), 0)
            h = jnp.where(pos_k <= pos_q, h, HIDDEN)
            th = jnp.tanh(h)
            a = (h + h * th).astype(BF16)
            a_t[index] = a
            g_t[index] = h
            return total + mm(kv_t[k, 64:128], a)

        total = lax.fori_loop(0, t + 1, inner, jnp.zeros((HEAD, 256), F32))
        y_t[2 * t] = total[:, :128]
        y_t[2 * t + 1] = total[:, 128:]
        return carry

    lax.fori_loop(0, 4, forward, 0)

    wait_recv(e_land.at[pl.ds(0, HEADS - 1)], 4)
    e_in = [e_land[i].astype(F32) for i in range(HEADS)]
    e_tiles = []
    for p in range(8):
        if p < 4:
            tile = jnp.where(lane_h, e_in[2 * p], swap(e_in[2 * p + 1]))
        else:
            tile = jnp.where(lane_h, swap(e_in[15 - 2 * p]), e_in[14 - 2 * p])
        e_tiles.append(tile[None])
    e_all = jnp.concatenate(e_tiles, axis=0)
    y_all = y_t[...]
    mean_h = jnp.sum(y_all, axis=1) * (1.0 / HEAD)
    spread = y_all - mean_h[:, None, :]
    stats = jnp.concatenate(
        [mean_h, jnp.sum(spread * spread, axis=1), jnp.sum(e_all * y_all, axis=1)], axis=0
    )
    stat_send[...] = stats
    stat_land[y] = stats
    to_heads(stat_send, stat_land, 6, False)

    def slopes(index, carry):
        h = g_t[index]
        th = jnp.tanh(h)
        g_t[index] = (1.0 + th) + h * (1.0 - th * th)
        return carry

    lax.fori_loop(0, 10, slopes, 0)

    wait_recv(stat_land.at[pl.ds(0, HEADS - 1)], 6)
    st = stat_land[...]
    means = st[:, 0:8]
    mean = jnp.sum(means, axis=0) * (1.0 / HEADS)
    off = means - mean[None]
    total = jnp.sum(st[:, 8:16], axis=0) + HEAD * jnp.sum(off * off, axis=0)
    rs2 = lax.rsqrt(total * (1.0 / WIDTH) + EPS)
    lean = rs2 * jnp.sum(st[:, 16:24], axis=0) * (1.0 / WIDTH)
    ny = (y_all - mean[:, None, :]) * rs2[:, None, :]
    dy = rs2[:, None, :] * (e_all - ny * lean[:, None, :])
    for p in range(8):
        tall = jnp.concatenate([jnp.zeros((HEAD, 128), F32), dy[p]], axis=0)
        dy_pad[128 * p : 128 * p + 128] = tall.T.astype(BF16)

    def by_source(tiles, i):
        if i % 2 == 0:
            return jnp.where(lane_h, tiles[i // 2], tiles[(15 - i) // 2])
        return swap(jnp.where(lane_h, tiles[(15 - i) // 2], tiles[i // 2]))

    for i in range(HEADS):
        ny_send[i] = by_source([ny[p] for p in range(8)], i).astype(BF16)
    to_heads(ny_send, ny_land, 7, True)
    ny_land[y] = ny_send[y]

    dq_t[...] = jnp.zeros_like(dq_t)

    def backward(k, first, step, count, fresh):
        span_k = pl.ds(512 * k, 512)
        kv = kv_nat[span_k]

        def inner(n, total):
            t = first + step * n
            index = t * (t + 1) // 2 + k
            span_q = pl.ds(pl.multiple_of(256 * t, 256), 256)
            dy_q = dy_pad[span_q]
            ds = (mm_t(kv, dy_q) * g_t[index]).astype(BF16)
            dq_t[t] += mm(kv_t[k, 0:64], ds)
            return total + mm(ds, q_pad[span_q]) + mm(a_t[index], dy_q)

        start = jnp.zeros((512, 128), F32) if fresh else dkv_s[span_k]
        dkv_s[span_k] = lax.fori_loop(0, count, inner, start)

    def both_halves(first, second):
        return jnp.concatenate(
            [
                dkv_s[pl.ds(pl.multiple_of(first * 64, 64), 64)],
                dkv_s[pl.ds(pl.multiple_of(second * 64, 64), 64)],
            ],
            axis=0,
        )

    def to_sibling(part):
        for i in range(4 * part, 4 * part + 4):
            sib_send[i] = both_halves(2 * i + 1 - core, 30 - 2 * i + core).astype(BF16)
        span = pl.ds(4 * part, 4)
        remote(sib_send.at[span], sib_land.at[span], 8, {"seq": sibling}, sib_sem.at[part]).start()

    def to_sources(part):
        span = pl.ds(4 * part, 4)
        pltpu.make_async_copy(sib_land.at[span], sib_land.at[span], sib_sem.at[part]).wait()
        for i in range(4 * part, 4 * part + 4):
            own = both_halves(2 * i + core, 31 - 2 * i - core) + sib_land[i].astype(F32)
            dkv_send[i] = own.astype(BF16)

        some_heads(dkv_send, dkv_land, 9, part)

    def some_heads(src, dst, k, part):
        def body(d, carry):
            peer = (y + far_first(d)) % HEADS

            @pl.when(peer // 4 == part)
            def _():
                remote(src.at[peer], dst.at[y], k, {"seq": 2 * peer + core}).start()

            return carry

        lax.fori_loop(0, HEADS - 1, body, 0)

    def queries_back(part):
        dq_tiles = []
        for t in range(4):
            if (t in (1, 2)) == (part == 1):
                both = dq_t[t] * 0.0625
                dq_tiles += [both[:, :128], both[:, 128:]]
            else:
                dq_tiles += [None, None]
        for i in range(4 * part, 4 * part + 4):
            dq_send[i] = by_source(dq_tiles, i).astype(BF16)
        some_heads(dq_send, dq_land, 13, part)

    backward(1, 1, 1, 3, True)
    backward(2, 2, 1, 2, True)
    to_sibling(1)
    backward(0, 1, 1, 2, True)
    queries_back(1)
    to_sources(1)
    backward(0, 0, 3, 2, False)
    backward(3, 3, 1, 1, True)
    to_sibling(0)
    queries_back(0)
    to_sources(0)
    wait_recv(ny_land.at[pl.ds(0, HEADS - 1)], 7)
    ny_full = ny_land[...].reshape(WIDTH, EVENTS).astype(F32)
    z_t = (ny_full * u_t[...]).astype(BF16)
    w_term[...] = mm(z_t, grad_s[...].astype(BF16)).reshape(N_TABLE, 16, WIDTH)
    w_sib_send[...] = w_term[pl.ds(pl.multiple_of(16 - 16 * core, 16), 16)].astype(BF16)
    remote(w_sib_send, w_sib_land, 18, {"seq": sibling}).start()
    d_u = (dz_t[...] * ny_full).T
    dq_land[y] = dq_send[y]
    dkv_land[y] = dkv_send[y]
    d_pre_u = (d_u * slope_s[:, 0:WIDTH]).astype(BF16)
    dn_u = mm_t(d_pre_u, w_in_v[:, 0:WIDTH])
    wait_recv(w_sib_land, 18)
    w_pair = w_term[pl.ds(pl.multiple_of(16 * core, 16), 16)] + w_sib_land[...].astype(F32)
    w_send[...] = w_pair.astype(BF16)

    def w_out_to_owner(n, carry):
        slot = (n + 8 + 4 * (me_t // 4 - 4 * core)) % 16
        peer = 16 * core + slot

        @pl.when(peer != me_t)
        def _():
            remote(w_send.at[slot], w_land.at[me_t], 10, {"table": peer}).start()

        return carry

    lax.fori_loop(0, 16, w_out_to_owner, 0)

    @pl.when(owns_w)
    def _():
        w_land[me_t] = w_send[me_t % 16]

    wait_recv(dkv_land.at[pl.ds(0, HEADS - 1)], 9)
    wait_recv(dq_land.at[pl.ds(0, HEADS - 1)], 13)
    d_k, d_v, d_q = [], [], []
    for p in range(4):
        first = dkv_land[2 * p].astype(F32)
        second = dkv_land[2 * p + 1].astype(F32)
        d_k.append(jnp.where(lane_e, first, swap(second)))
        d_v.append(jnp.where(lane_e, swap(first), second))
        pair = [dq_land[2 * p + n].astype(F32) for n in range(2)]
        d_q.append(jnp.concatenate(pair, axis=0).T)
    d_proj = jnp.concatenate(d_v + d_q + d_k, axis=1)
    d_pre = (d_proj * slope_s[:, WIDTH:]).astype(BF16)
    dn = dn_u + mm_t(d_pre, w_in_v[:, WIDTH:])
    nx = nx_s[...]
    first = jnp.mean(dn, axis=1, keepdims=True)
    second = jnp.mean(dn * nx, axis=1, keepdims=True)
    d_x = grad_s[...] + rs1 * (dn - first - nx * second)

    place_t = one_hot(iota((SLOTS, EVENTS), 0) == slot_row)
    dx_send[...] = stack_halves(mm(place_t, d_x.astype(BF16)))
    to_table_group(dx_send, dx_land, 11, 1)
    to_table_group(dx_send, dx_land, 16, 0)
    dx_land[me_t] = dx_send[me_t]

    @pl.when(owns_w)
    def _():
        wait_recv(w_land.at[pl.ds(0, N_TABLE - 1)], 10)
        part = jnp.sum(w_land[...].astype(F32), axis=0).astype(BF16)
        part_send[...] = part
        part_land[y] = part

        def body(d, carry):
            peer = 2 * ((y + far_first(d // 2)) % HEADS) + (core + 1 + d) % 2
            remote(part_send, part_land.at[y], 12, {"seq": peer}).start()
            return carry

        lax.fori_loop(0, N_SEQ - 1, body, 0)

    group = iota((32, 128), 1) >> 5
    spread_of = iota((128, WIDTH), 1)
    spread_to = one_hot(
        iota((128, WIDTH), 0) == 32 * (spread_of >> 7) + (spread_of & 31)
    )

    def columns(side):
        planes = [
            dx_land[pl.ds(pl.multiple_of(4 * ((me_t // 4 + 6 + n) % 8), 4), 4)].astype(F32)
            for n in range(4 * side, 4 * side + 4)
        ]
        for part in range(2):
            rows = [plane[:, 8 * part : 8 * part + 8].reshape(32, 256) for plane in planes]
            for tile in range(2):
                cuts = [row[:, 128 * tile : 128 * tile + 128] for row in rows]
                for g in range(4):
                    chunk = None
                    for q in range(4):
                        shift = 32 * ((q - g) % 4)
                        cut = pltpu.roll(cuts[q], shift, 1) if shift else cuts[q]
                        chunk = cut if q == 0 else jnp.where(group == q, cut, chunk)
                    col_send[side, 8 * part + 4 * tile + g] = chunk.astype(BF16)
        to_seq(col_send.at[side], col_land.at[side], 15 if side == 0 else 17, True)
        col_land[side, me_s] = col_send[side, me_s]

    def placed(side, total):
        wide = mm(col_land[side].reshape(N_SEQ * 32, 128), spread_to)
        for q in range(4):
            n = 4 * side + q
            put = (wide[:, 128 * q : 128 * q + 128] * mask_lo[n]).astype(BF16)
            hot_q = jnp.concatenate([hot_hi[n, quad] for quad in range(N_SEQ // 4)], axis=1)
            total = total + mm(hot_q, put)
        return total

    wait_recv(dx_land.at[pl.ds(0, 15)], 11)
    columns(0)
    wait_recv(dx_land.at[pl.ds(0, 16)], 16)
    columns(1)

    @pl.when(owns_w)
    def _():
        wait_recv(part_land.at[pl.ds(0, HEADS - 1)], 12)

    @pl.when(jnp.logical_not(owns_w))
    def _():
        wait_recv(part_land, 12)

    w_grad_ref[...] = jnp.sum(part_land[...].astype(F32), axis=0)

    wait_recv(col_land.at[0, pl.ds(0, N_SEQ - 1)], 15)
    total = placed(0, jnp.zeros((256, 128), F32))
    wait_recv(col_land.at[1, pl.ds(0, N_SEQ - 1)], 17)
    total = placed(1, total)
    turned = total.T
    for k in range(4):
        out_ref[:, 256 * k : 256 * k + 256] = turned[32 * k : 32 * k + 32]

    wait_sent(ids_land.at[pl.ds(0, N_TABLE - 1)], 0)
    wait_sent(fetch_send.at[pl.ds(0, N_TABLE - 1)], 1)
    wait_sent(slot_land.at[pl.ds(0, N_SEQ - 1)], 2)
    wait_sent(kv_send.at[pl.ds(0, HEADS - 1)], 3)
    wait_sent(q_send.at[pl.ds(0, HEADS - 1)], 14)
    wait_sent(e_send.at[pl.ds(0, HEADS - 1)], 4)
    wait_sent(kv_sib, 5)
    wait_sent(stat_land.at[pl.ds(0, HEADS - 1)], 6)
    wait_sent(ny_send.at[pl.ds(0, HEADS - 1)], 7)
    wait_sent(sib_send, 8)
    wait_sent(dkv_send.at[pl.ds(0, HEADS - 1)], 9)
    wait_sent(dq_send.at[pl.ds(0, HEADS - 1)], 13)
    wait_sent(w_sib_send, 18)

    @pl.when(owns_w)
    def _():
        wait_sent(w_send.at[pl.ds(0, 15)], 10)
        wait_sent(w_land.at[pl.ds(0, N_SEQ - 1)], 12)

    @pl.when(jnp.logical_not(owns_w))
    def _():
        wait_sent(w_send, 10)

    wait_sent(dx_send.at[pl.ds(0, 15)], 11)
    wait_sent(dx_send.at[pl.ds(0, 16)], 16)
    wait_sent(col_send.at[0, pl.ds(0, N_SEQ - 1)], 15)
    wait_sent(col_send.at[1, pl.ds(0, N_SEQ - 1)], 17)


def on_device(table, item_rows, lengths, w_in, w_out, cotangent):
    vmem = pl.BlockSpec(memory_space=pltpu.VMEM)
    smem = pl.BlockSpec(memory_space=pltpu.SMEM)
    anywhere = pl.BlockSpec(memory_space=pl.ANY)
    buf = pltpu.VMEM
    scratch = [
        buf((ROWS_T, WIDTH), BF16),
        buf((WIDTH, 4 * WIDTH), BF16),
        buf((WIDTH, WIDTH), BF16),
        buf((EVENTS, WIDTH), BF16),
        buf((1, EVENTS), I32),
        buf((N_TABLE, 1, EVENTS), I32),
        buf((N_TABLE, 16, 256), BF16),
        buf((N_TABLE, 16, 256), BF16),
        buf((8, 128), F32),
        buf((N_SEQ, 8, 128), F32),
        buf((HEADS, 128, 128), BF16),
        buf((HEADS, 128, 128), BF16),
        buf((HEADS, HEAD, 128), BF16),
        buf((HEADS, HEAD, 128), BF16),
        buf((HEADS, 128, 128), BF16),
        buf((HEADS, HEAD, 128), BF16),
        buf((HEADS, HEAD, 128), BF16),
        buf((24, 128), F32),
        buf((HEADS, 24, 128), F32),
        buf((HEADS, HEAD, 128), BF16),
        buf((HEADS, HEAD, 128), BF16),
        buf((N_TABLE, 16, WIDTH), F32),
        buf((16, 16, WIDTH), BF16),
        buf((16, 16, WIDTH), BF16),
        buf((16, 16, WIDTH), BF16),
        buf((N_TABLE, 16, WIDTH), BF16),
        buf((16, WIDTH), BF16),
        buf((HEADS, 16, WIDTH), BF16),
        buf((HEADS, 128, 128), BF16),
        buf((HEADS, 128, 128), BF16),
        buf((HEADS, 128, 128), BF16),
        buf((HEADS, 128, 128), BF16),
        buf((HEADS, HEAD, 128), BF16),
        buf((HEADS, HEAD, 128), BF16),
        buf((N_TABLE, 16, 256), BF16),
        buf((N_TABLE, 16, 256), BF16),
        buf((2, N_SEQ, 32, 128), BF16),
        buf((2, N_SEQ, 32, 128), BF16),
        buf((EVENTS, WIDTH), F32),
        buf((WIDTH, EVENTS), F32),
        buf((WIDTH, EVENTS), F32),
        buf((EVENTS, WIDTH), F32),
        buf((EVENTS, 4 * WIDTH), F32),
        buf((2048, 128), BF16),
        buf((4, 128, 512), BF16),
        buf((1024, 128), BF16),
        buf((1024, 128), BF16),
        buf((10, 512, 256), BF16),
        buf((10, 512, 256), F32),
        buf((8, HEAD, 128), F32),
        buf((4, HEAD, 256), F32),
        buf((2048, 128), F32),
        buf((8, N_SEQ // 4, 256, 128), BF16),
        buf((8, N_SEQ * 32, 128), F32),
        buf((SLOTS, 128), F32),
        pltpu.SemaphoreType.DMA((5,)),
        pltpu.SemaphoreType.DMA((19,)),
        pltpu.SemaphoreType.DMA((19,)),
        pltpu.SemaphoreType.DMA((HEADS,)),
        pltpu.SemaphoreType.DMA((2,)),
    ]
    sums, w_grad = pl.pallas_call(
        kernel,
        out_shape=(
            pltpu.VMEM((32, ROWS_T), F32),
            pltpu.VMEM((16, WIDTH), F32),
        ),
        in_specs=[anywhere, smem, anywhere, anywhere, anywhere, anywhere],
        out_specs=(vmem, vmem),
        scratch_shapes=scratch,
        compiler_params=pltpu.CompilerParams(
            collective_id=0, has_side_effects=True, vmem_limit_bytes=56 * 1024 * 1024
        ),
    )(item_rows, lengths, cotangent[0], table, w_in, w_out)
    return sums.T, w_grad


def solution(mesh):
    return jax.shard_map(
        on_device,
        mesh=mesh,
        in_specs=(
            P("table", None),
            P("table", "seq"),
            P("table"),
            P(),
            P(),
            P("table", "seq", None),
        ),
        out_specs=(P("table", "seq"), P("table", None)),
        check_vma=False,
    )
```

```python
import jax
import jax.numpy as jnp
from jax import lax
from jax.experimental import pallas as pl
from jax.experimental.pallas import tpu as pltpu
from jax.sharding import PartitionSpec as P

EPS = 1e-05
MESH = pl.DeviceIdType.MESH
F32 = jnp.float32
BF16 = jnp.bfloat16
I32 = jnp.int32

N_SEQ = 16
N_TABLE = 32
EVENTS = 128
WIDTH = 512
HEADS = 8
HEAD = 64
CAP = 8
ROWS_T = 1024
SLOTS = N_TABLE * CAP
HIDDEN = -64.0


def mm(a, b):
    return jnp.dot(a, b, preferred_element_type=F32)


def mm_t(a, b):
    return lax.dot_general(a, b, (((1,), (1,)), ((), ())), preferred_element_type=F32)


def iota(shape, dim):
    return lax.broadcasted_iota(I32, shape, dim)


def one_hot(mask):
    return jnp.where(mask, 1.0, 0.0).astype(BF16)


def swap(tile):
    return pltpu.roll(tile, 64, tile.ndim - 1)


def left(shape):
    return iota(shape, len(shape) - 1) < 64


def kernel(
    rows_hbm,
    len_ref,
    cot_hbm,
    table_hbm,
    w_in_hbm,
    w_out_hbm,
    out_ref,
    w_grad_ref,
    table_v,
    w_in_v,
    w_out_v,
    cot_v,
    rows_v,
    ids_land,
    fetch_send,
    fetch_land,
    slot_send,
    slot_land,
    kv_send,
    kv_own,
    q_send,
    q_land,
    kv_sib,
    e_send,
    e_land,
    stat_send,
    stat_land,
    ny_send,
    ny_land,
    w_term,
    w_sib_send,
    w_sib_land,
    w_send,
    w_land,
    part_send,
    part_land,
    sib_send,
    sib_land,
    dkv_send,
    dkv_land,
    dq_send,
    dq_land,
    dx_send,
    dx_land,
    col_send,
    col_land,
    grad_s,
    dz_t,
    u_t,
    nx_s,
    slope_s,
    kv_nat,
    kv_t,
    q_pad,
    dy_pad,
    a_t,
    g_t,
    y_t,
    dq_t,
    dkv_s,
    hot_hi,
    mask_lo,
    asked_s,
    load_sem,
    send_sem,
    recv_sem,
    kv_sem,
    sib_sem,
):
    me_s = lax.axis_index("seq")
    me_t = lax.axis_index("table")
    y = me_s // 2
    core = me_s % 2
    sibling = me_s + 1 - 2 * core
    owns_w = core == me_t // 16

    loads = [
        pltpu.make_async_copy(src, dst, load_sem.at[k])
        for k, (src, dst) in enumerate(
            (
                (rows_hbm, rows_v),
                (table_hbm, table_v),
                (cot_hbm, cot_v),
                (w_out_hbm, w_out_v),
                (w_in_hbm, w_in_v),
            )
        )
    ]
    for load in loads:
        load.start()

    barrier = pltpu.get_barrier_semaphore()

    def greet_table(d, carry):
        pl.semaphore_signal(
            barrier, inc=1, device_id={"table": (me_t + d) % N_TABLE}, device_id_type=MESH
        )
        return carry

    def greet_seq(d, carry):
        pl.semaphore_signal(
            barrier, inc=1, device_id={"seq": (me_s + d) % N_SEQ}, device_id_type=MESH
        )
        return carry

    lax.fori_loop(1, N_TABLE, greet_table, 0)
    lax.fori_loop(1, N_SEQ, greet_seq, 0)

    def remote(src, dst, k, where, recv=None):
        return pltpu.make_async_remote_copy(
            src_ref=src,
            dst_ref=dst,
            send_sem=send_sem.at[k],
            recv_sem=recv_sem.at[k] if recv is None else recv,
            device_id=where,
            device_id_type=MESH,
        )

    def far_first(n):
        return 4 + ((n + 1) // 2) * (2 * (n % 2) - 1)

    def to_table(src, dst, k, split):
        def body(d, carry):
            peer = (me_t + d) % N_TABLE
            remote(src.at[peer] if split else src, dst.at[me_t], k, {"table": peer}).start()
            return carry

        lax.fori_loop(1, N_TABLE, body, 0)

    def to_table_group(src, dst, k, group):
        def body(d, carry):
            z = (me_t // 4 + far_first(d // 4)) % 8
            x = (me_t + 2 + ((d % 4 + 1) // 2) * (2 * (d % 2) - 1)) % 4
            peer = 4 * z + x
            remote(src.at[peer], dst.at[me_t], k, {"table": peer}).start()
            return carry

        lax.fori_loop(16 * group, 16 + 15 * group, body, 0)

    def to_seq(src, dst, k, split):
        def body(d, carry):
            peer = 2 * ((y + far_first(d // 2)) % HEADS) + (core + 1 + d) % 2
            remote(src.at[peer] if split else src, dst.at[me_s], k, {"seq": peer}).start()
            return carry

        lax.fori_loop(0, N_SEQ - 1, body, 0)

    def to_heads(src, dst, k, split, sems=None):
        def body(d, carry):
            peer = (y + far_first(d)) % HEADS
            recv = None if sems is None else sems.at[y]
            remote(
                src.at[peer] if split else src, dst.at[y], k, {"seq": 2 * peer + core}, recv
            ).start()
            return carry

        lax.fori_loop(0, HEADS - 1, body, 0)

    def wait_recv(ref, k):
        pltpu.make_async_copy(ref, ref, recv_sem.at[k]).wait()

    def wait_sent(ref, k):
        pltpu.make_async_copy(ref, ref, send_sem.at[k]).wait()

    def z_rows(n):
        return pl.multiple_of(32 * ((me_t // 4 + 6 + n) % 8), 32)

    loads[0].wait()
    ids_row = rows_v[...]
    ids_land[me_t] = ids_row
    pl.semaphore_wait(barrier, N_TABLE - 1 + N_SEQ - 1)
    to_table(rows_v, ids_land, 0, False)

    square = (EVENTS, EVENTS)
    row_of, col_of = iota(square, 0), iota(square, 1)
    ids_wide = jnp.broadcast_to(ids_row, square)
    ids_col = jnp.sum(
        jnp.where(row_of == col_of, ids_wide.astype(F32), 0.0), axis=1, keepdims=True
    ).astype(I32)
    owner_row = ids_wide >> 10
    owner_col = jnp.broadcast_to(ids_col >> 10, square)
    same = owner_row == owner_col
    rank_col = jnp.sum(
        jnp.where(same & (col_of < row_of), 1.0, 0.0), axis=1, keepdims=True
    ).astype(I32)
    rank_row = jnp.sum(
        jnp.where(same & (row_of < col_of), 1.0, 0.0), axis=0, keepdims=True
    ).astype(I32)
    slot_col = (ids_col >> 10) * 16 + rank_col
    slot_row = (ids_row >> 10) * CAP + rank_row

    half = iota((EVENTS, 1), 0)
    span = jnp.where(half < 64, me_s, 2 * N_SEQ - 1 - me_s)
    live = (span * 64 + (half & 63)) < len_ref[0]
    loads[2].wait()
    grad = jnp.where(live, cot_v[...].astype(F32), 0.0)
    grad_b = grad.astype(BF16)
    grad_s[...] = grad
    loads[3].wait()
    dz_t[...] = mm_t(w_out_v[...], grad_b)

    wait_recv(ids_land.at[pl.ds(0, N_TABLE - 1)], 0)
    ids = jnp.broadcast_to(ids_land[...], (N_TABLE, CAP, EVENTS)).reshape(SLOTS, EVENTS)
    mine = (ids >> 10) == me_t
    before = one_hot(row_of < col_of)
    rank = mm(one_hot(mine), before)
    turn = (iota((SLOTS, EVENTS), 0) & 7).astype(F32)
    picked = jnp.where(mine & (rank == turn), (ids & 1023).astype(F32) + 1.0, 0.0)
    asked = jnp.sum(picked, axis=1, keepdims=True) - 1.0
    loads[1].wait()
    hot = one_hot(iota((SLOTS, ROWS_T), 1) == asked.astype(I32))

    def stack_halves(values):
        cut = values.reshape(N_TABLE, CAP, WIDTH)
        return jnp.concatenate([cut[:, :, :256], cut[:, :, 256:]], axis=1).astype(BF16)

    fetch_send[...] = stack_halves(mm(hot, table_v[...]))
    to_table(fetch_send, fetch_land, 1, True)
    fetch_land[me_t] = fetch_send[me_t]

    asked_s[...] = jnp.broadcast_to(asked, (SLOTS, 128))
    tiles = []
    for n in range(8):
        piece = asked_s[pl.ds(z_rows(n), 32)]
        tiles.append(jnp.concatenate([piece] * 4, axis=0).T[0:1])
    slots = jnp.concatenate(tiles, axis=0)
    slot_send[...] = slots
    slot_land[me_s] = slots
    to_seq(slot_send, slot_land, 2, False)

    place = iota((EVENTS, 2 * SLOTS), 1)
    pick_lo = one_hot(place == slot_col)
    pick_hi = one_hot(place == slot_col + CAP)
    loads[4].wait()
    wait_recv(fetch_land.at[pl.ds(0, N_TABLE - 1)], 1)
    fetched = fetch_land[...].reshape(2 * SLOTS, 256)
    emb = jnp.concatenate([mm(pick_lo, fetched), mm(pick_hi, fetched)], axis=1)

    center = emb - jnp.mean(emb, axis=1, keepdims=True)
    rs1 = lax.rsqrt(jnp.mean(center * center, axis=1, keepdims=True) + EPS)
    nx = center * rs1
    nx_s[...] = nx
    normed = nx.astype(BF16)

    def project(k):
        cols = slice(WIDTH * k, WIDTH * k + WIDTH)
        pre = mm(normed, w_in_v[:, cols])
        sigma = 0.5 + 0.5 * jnp.tanh(0.5 * pre)
        slope_s[:, cols] = sigma * (1.0 + pre * (1.0 - sigma))
        return (pre * sigma).astype(BF16).astype(F32)

    lane_e = left((EVENTS, 128))
    lane_h = left((HEAD, 128))
    keys, values = project(3), project(1)
    for p in range(4):
        cols = slice(128 * p, 128 * p + 128)
        kt, vt = keys[:, cols], values[:, cols]
        kv_send[2 * p] = jnp.where(lane_e, kt, swap(vt)).astype(BF16)
        kv_send[2 * p + 1] = jnp.where(lane_e, swap(kt), vt).astype(BF16)
    to_heads(kv_send, kv_own, 3, True, kv_sem)
    kv_own[y] = kv_send[y]
    queries = project(2) * 0.0625
    for p in range(4):
        cols = slice(128 * p, 128 * p + 128)
        q_lo, q_hi = queries[:64, cols], queries[64:, cols]
        q_send[2 * p] = jnp.where(lane_h, q_lo, swap(q_hi)).astype(BF16)
        q_send[2 * p + 1] = jnp.where(lane_h, swap(q_lo), q_hi).astype(BF16)
    to_heads(q_send, q_land, 14, True)
    q_land[y] = q_send[y]
    gate = project(0)
    gate_t = gate.T
    u_t[...] = gate_t
    e_full = dz_t[...] * gate_t
    e_full = e_full - jnp.mean(e_full, axis=0, keepdims=True)
    e_send[...] = e_full.reshape(HEADS, HEAD, EVENTS).astype(BF16)
    to_heads(e_send, e_land, 4, True)
    e_land[y] = e_send[y]

    wait_recv(slot_land.at[pl.ds(0, N_SEQ - 1)], 2)
    part_8 = iota((8, 128), 1) >> 5

    def prepare(quad, carry):
        four = slot_land[4 * quad]
        for n in range(1, 4):
            four = jnp.where(part_8 == n, slot_land[4 * quad + n], four)
        four = four.astype(I32)
        span_rows = pl.ds(pl.multiple_of(128 * quad, 128), 128)
        for n in range(8):
            line = four[n : n + 1]
            hot_hi[n, quad] = one_hot(iota((256, 128), 0) == (line & 255))
            column = jnp.broadcast_to((line >> 8).astype(F32), square).T
            mask_lo[n, span_rows] = jnp.where((col_of >> 5).astype(F32) == column, 1.0, 0.0)
        return carry

    lax.fori_loop(0, N_SEQ // 4, prepare, 0)

    def pass_on(d, carry):
        peer = (y + jnp.where(d == 0, 0, far_first(d - 1))) % HEADS

        @pl.when(d > 0)
        def _():
            pltpu.make_async_copy(kv_own.at[peer], kv_own.at[peer], kv_sem.at[peer]).wait()

        remote(kv_own.at[peer], kv_sib.at[peer], 5, {"seq": sibling}).start()
        return carry

    lax.fori_loop(0, HEADS, pass_on, 0)

    for i in range(HEADS):
        block = kv_own[i]
        kv_nat[pl.ds(pl.multiple_of((2 * i + core) * 64, 64), 64)] = block[0:64]
        kv_nat[pl.ds(pl.multiple_of((31 - 2 * i - core) * 64, 64), 64)] = block[64:128]
    wait_recv(kv_sib, 5)
    for i in range(HEADS):
        block = kv_sib[i]
        kv_nat[pl.ds(pl.multiple_of((2 * i + 1 - core) * 64, 64), 64)] = block[0:64]
        kv_nat[pl.ds(pl.multiple_of((30 - 2 * i + core) * 64, 64), 64)] = block[64:128]
    for k in range(4):
        kv_t[k] = kv_nat[512 * k : 512 * k + 512].T
    wait_recv(q_land.at[pl.ds(0, HEADS - 1)], 14)
    for i in range(HEADS):
        packed = q_land[i].astype(F32)
        q_pad[64 * i : 64 * i + 64] = jnp.where(lane_h, packed, 0.0).astype(BF16)
        q_pad[64 * (15 - i) : 64 * (16 - i)] = jnp.where(lane_h, swap(packed), 0.0).astype(BF16)

    def forward(t, carry):
        q = q_pad[pl.ds(pl.multiple_of(256 * t, 256), 256)]
        lane = 256 * t + iota((1, 256), 1)
        block_q = lane >> 6
        block_q = 2 * block_q + jnp.where(block_q < 8, core, 1 - core)
        pos_q = block_q * 64 + (lane & 63)

        def inner(k, total):
            index = t * (t + 1) // 2 + k
            kv = kv_nat[pl.ds(pl.multiple_of(512 * k, 512), 512)]
            h = mm_t(kv, q)
            pos_k = 512 * k + iota((512, 1), 0)
            h = jnp.where(pos_k <= pos_q, h, HIDDEN)
            th = jnp.tanh(h)
            a = (h + h * th).astype(BF16)
            a_t[index] = a
            g_t[index] = h
            return total + mm(kv_t[k, 64:128], a)

        total = lax.fori_loop(0, t + 1, inner, jnp.zeros((HEAD, 256), F32))
        y_t[2 * t] = total[:, :128]
        y_t[2 * t + 1] = total[:, 128:]
        return carry

    lax.fori_loop(0, 4, forward, 0)

    wait_recv(e_land.at[pl.ds(0, HEADS - 1)], 4)
    e_in = [e_land[i].astype(F32) for i in range(HEADS)]
    e_tiles = []
    for p in range(8):
        if p < 4:
            tile = jnp.where(lane_h, e_in[2 * p], swap(e_in[2 * p + 1]))
        else:
            tile = jnp.where(lane_h, swap(e_in[15 - 2 * p]), e_in[14 - 2 * p])
        e_tiles.append(tile[None])
    e_all = jnp.concatenate(e_tiles, axis=0)
    y_all = y_t[...]
    mean_h = jnp.sum(y_all, axis=1) * (1.0 / HEAD)
    spread = y_all - mean_h[:, None, :]
    stats = jnp.concatenate(
        [mean_h, jnp.sum(spread * spread, axis=1), jnp.sum(e_all * y_all, axis=1)], axis=0
    )
    stat_send[...] = stats
    stat_land[y] = stats
    to_heads(stat_send, stat_land, 6, False)

    def slopes(index, carry):
        h = g_t[index]
        th = jnp.tanh(h)
        g_t[index] = (1.0 + th) + h * (1.0 - th * th)
        return carry

    lax.fori_loop(0, 10, slopes, 0)

    wait_recv(stat_land.at[pl.ds(0, HEADS - 1)], 6)
    st = stat_land[...]
    means = st[:, 0:8]
    mean = jnp.sum(means, axis=0) * (1.0 / HEADS)
    off = means - mean[None]
    total = jnp.sum(st[:, 8:16], axis=0) + HEAD * jnp.sum(off * off, axis=0)
    rs2 = lax.rsqrt(total * (1.0 / WIDTH) + EPS)
    lean = rs2 * jnp.sum(st[:, 16:24], axis=0) * (1.0 / WIDTH)
    ny = (y_all - mean[:, None, :]) * rs2[:, None, :]
    dy = rs2[:, None, :] * (e_all - ny * lean[:, None, :])
    for p in range(8):
        tall = jnp.concatenate([jnp.zeros((HEAD, 128), F32), dy[p]], axis=0)
        dy_pad[128 * p : 128 * p + 128] = tall.T.astype(BF16)

    def by_source(tiles, i):
        if i % 2 == 0:
            return jnp.where(lane_h, tiles[i // 2], tiles[(15 - i) // 2])
        return swap(jnp.where(lane_h, tiles[(15 - i) // 2], tiles[i // 2]))

    for i in range(HEADS):
        ny_send[i] = by_source([ny[p] for p in range(8)], i).astype(BF16)
    to_heads(ny_send, ny_land, 7, True)
    ny_land[y] = ny_send[y]

    dq_t[...] = jnp.zeros_like(dq_t)

    def backward(k, first, step, count, fresh):
        span_k = pl.ds(512 * k, 512)
        kv = kv_nat[span_k]

        def inner(n, total):
            t = first + step * n
            index = t * (t + 1) // 2 + k
            span_q = pl.ds(pl.multiple_of(256 * t, 256), 256)
            dy_q = dy_pad[span_q]
            ds = (mm_t(kv, dy_q) * g_t[index]).astype(BF16)
            dq_t[t] += mm(kv_t[k, 0:64], ds)
            return total + mm(ds, q_pad[span_q]) + mm(a_t[index], dy_q)

        start = jnp.zeros((512, 128), F32) if fresh else dkv_s[span_k]
        dkv_s[span_k] = lax.fori_loop(0, count, inner, start)

    def both_halves(first, second):
        return jnp.concatenate(
            [
                dkv_s[pl.ds(pl.multiple_of(first * 64, 64), 64)],
                dkv_s[pl.ds(pl.multiple_of(second * 64, 64), 64)],
            ],
            axis=0,
        )

    def to_sibling(part):
        for i in range(4 * part, 4 * part + 4):
            sib_send[i] = both_halves(2 * i + 1 - core, 30 - 2 * i + core).astype(BF16)
        span = pl.ds(4 * part, 4)
        remote(sib_send.at[span], sib_land.at[span], 8, {"seq": sibling}, sib_sem.at[part]).start()

    def to_sources(part):
        span = pl.ds(4 * part, 4)
        pltpu.make_async_copy(sib_land.at[span], sib_land.at[span], sib_sem.at[part]).wait()
        for i in range(4 * part, 4 * part + 4):
            own = both_halves(2 * i + core, 31 - 2 * i - core) + sib_land[i].astype(F32)
            dkv_send[i] = own.astype(BF16)

        some_heads(dkv_send, dkv_land, 9, part)

    def some_heads(src, dst, k, part):
        def body(d, carry):
            peer = (y + far_first(d)) % HEADS

            @pl.when(peer // 4 == part)
            def _():
                remote(src.at[peer], dst.at[y], k, {"seq": 2 * peer + core}).start()

            return carry

        lax.fori_loop(0, HEADS - 1, body, 0)

    def queries_back(part):
        dq_tiles = []
        for t in range(4):
            if (t in (1, 2)) == (part == 1):
                both = dq_t[t] * 0.0625
                dq_tiles += [both[:, :128], both[:, 128:]]
            else:
                dq_tiles += [None, None]
        for i in range(4 * part, 4 * part + 4):
            dq_send[i] = by_source(dq_tiles, i).astype(BF16)
        some_heads(dq_send, dq_land, 13, part)

    backward(1, 1, 1, 3, True)
    backward(2, 2, 1, 2, True)
    to_sibling(1)
    backward(0, 1, 1, 2, True)
    queries_back(1)
    to_sources(1)
    backward(0, 0, 3, 2, False)
    backward(3, 3, 1, 1, True)
    to_sibling(0)
    queries_back(0)
    to_sources(0)
    wait_recv(ny_land.at[pl.ds(0, HEADS - 1)], 7)
    ny_full = ny_land[...].reshape(WIDTH, EVENTS).astype(F32)
    z_t = (ny_full * u_t[...]).astype(BF16)
    w_term[...] = mm(z_t, grad_s[...].astype(BF16)).reshape(N_TABLE, 16, WIDTH)
    w_sib_send[...] = w_term[pl.ds(pl.multiple_of(16 - 16 * core, 16), 16)].astype(BF16)
    remote(w_sib_send, w_sib_land, 18, {"seq": sibling}).start()
    d_u = (dz_t[...] * ny_full).T
    dq_land[y] = dq_send[y]
    dkv_land[y] = dkv_send[y]
    d_pre_u = (d_u * slope_s[:, 0:WIDTH]).astype(BF16)
    dn_u = mm_t(d_pre_u, w_in_v[:, 0:WIDTH])
    wait_recv(w_sib_land, 18)
    w_pair = w_term[pl.ds(pl.multiple_of(16 * core, 16), 16)] + w_sib_land[...].astype(F32)
    w_send[...] = w_pair.astype(BF16)

    def w_out_to_owner(n, carry):
        slot = (n + 8 + 4 * (me_t // 4 - 4 * core)) % 16
        peer = 16 * core + slot

        @pl.when(peer != me_t)
        def _():
            remote(w_send.at[slot], w_land.at[me_t], 10, {"table": peer}).start()

        return carry

    lax.fori_loop(0, 16, w_out_to_owner, 0)

    @pl.when(owns_w)
    def _():
        w_land[me_t] = w_send[me_t % 16]

    place_t = one_hot(iota((SLOTS, EVENTS), 0) == slot_row)
    wait_recv(dq_land.at[pl.ds(0, HEADS - 1)], 13)
    d_q = dq_land[...].reshape(WIDTH, EVENTS).astype(F32).T
    d_pre_q = (d_q * slope_s[:, 2 * WIDTH : 3 * WIDTH]).astype(BF16)
    dn_q = dn_u + mm_t(d_pre_q, w_in_v[:, 2 * WIDTH : 3 * WIDTH])
    wait_recv(dkv_land.at[pl.ds(0, HEADS - 1)], 9)
    d_k, d_v = [], []
    for p in range(4):
        first = dkv_land[2 * p].astype(F32)
        second = dkv_land[2 * p + 1].astype(F32)
        d_k.append(jnp.where(lane_e, first, swap(second)))
        d_v.append(jnp.where(lane_e, swap(first), second))
    d_pre_v = (jnp.concatenate(d_v, axis=1) * slope_s[:, WIDTH : 2 * WIDTH]).astype(BF16)
    d_pre_k = (jnp.concatenate(d_k, axis=1) * slope_s[:, 3 * WIDTH :]).astype(BF16)
    dn = dn_q + mm_t(d_pre_v, w_in_v[:, WIDTH : 2 * WIDTH])
    dn = dn + mm_t(d_pre_k, w_in_v[:, 3 * WIDTH :])
    nx = nx_s[...]
    first = jnp.mean(dn, axis=1, keepdims=True)
    second = jnp.mean(dn * nx, axis=1, keepdims=True)
    d_x = grad_s[...] + rs1 * (dn - first - nx * second)

    dx_send[...] = stack_halves(mm(place_t, d_x.astype(BF16)))
    to_table_group(dx_send, dx_land, 11, 1)
    to_table_group(dx_send, dx_land, 16, 0)
    dx_land[me_t] = dx_send[me_t]

    @pl.when(owns_w)
    def _():
        wait_recv(w_land.at[pl.ds(0, N_TABLE - 1)], 10)
        part = jnp.sum(w_land[...].astype(F32), axis=0).astype(BF16)
        part_send[...] = part
        part_land[y] = part

        def body(d, carry):
            peer = 2 * ((y + far_first(d // 2)) % HEADS) + (core + 1 + d) % 2
            remote(part_send, part_land.at[y], 12, {"seq": peer}).start()
            return carry

        lax.fori_loop(0, N_SEQ - 1, body, 0)

    group = iota((32, 128), 1) >> 5
    spread_of = iota((128, WIDTH), 1)
    spread_to = one_hot(
        iota((128, WIDTH), 0) == 32 * (spread_of >> 7) + (spread_of & 31)
    )

    def columns(side):
        planes = [
            dx_land[pl.ds(pl.multiple_of(4 * ((me_t // 4 + 6 + n) % 8), 4), 4)].astype(F32)
            for n in range(4 * side, 4 * side + 4)
        ]
        for part in range(2):
            rows = [plane[:, 8 * part : 8 * part + 8].reshape(32, 256) for plane in planes]
            for tile in range(2):
                cuts = [row[:, 128 * tile : 128 * tile + 128] for row in rows]
                for g in range(4):
                    chunk = None
                    for q in range(4):
                        shift = 32 * ((q - g) % 4)
                        cut = pltpu.roll(cuts[q], shift, 1) if shift else cuts[q]
                        chunk = cut if q == 0 else jnp.where(group == q, cut, chunk)
                    col_send[side, 8 * part + 4 * tile + g] = chunk.astype(BF16)
        to_seq(col_send.at[side], col_land.at[side], 15 if side == 0 else 17, True)
        col_land[side, me_s] = col_send[side, me_s]

    def placed(side, total):
        wide = mm(col_land[side].reshape(N_SEQ * 32, 128), spread_to)
        for q in range(4):
            n = 4 * side + q
            put = (wide[:, 128 * q : 128 * q + 128] * mask_lo[n]).astype(BF16)
            hot_q = jnp.concatenate([hot_hi[n, quad] for quad in range(N_SEQ // 4)], axis=1)
            total = total + mm(hot_q, put)
        return total

    wait_recv(dx_land.at[pl.ds(0, 15)], 11)
    columns(0)
    wait_recv(dx_land.at[pl.ds(0, 16)], 16)
    columns(1)

    @pl.when(owns_w)
    def _():
        wait_recv(part_land.at[pl.ds(0, HEADS - 1)], 12)

    @pl.when(jnp.logical_not(owns_w))
    def _():
        wait_recv(part_land, 12)

    w_grad_ref[...] = jnp.sum(part_land[...].astype(F32), axis=0)

    wait_recv(col_land.at[0, pl.ds(0, N_SEQ - 1)], 15)
    total = placed(0, jnp.zeros((256, 128), F32))
    wait_recv(col_land.at[1, pl.ds(0, N_SEQ - 1)], 17)
    total = placed(1, total)
    turned = total.T
    for k in range(4):
        out_ref[:, 256 * k : 256 * k + 256] = turned[32 * k : 32 * k + 32]

    wait_sent(ids_land.at[pl.ds(0, N_TABLE - 1)], 0)
    wait_sent(fetch_send.at[pl.ds(0, N_TABLE - 1)], 1)
    wait_sent(slot_land.at[pl.ds(0, N_SEQ - 1)], 2)
    wait_sent(kv_send.at[pl.ds(0, HEADS - 1)], 3)
    wait_sent(q_send.at[pl.ds(0, HEADS - 1)], 14)
    wait_sent(e_send.at[pl.ds(0, HEADS - 1)], 4)
    wait_sent(kv_sib, 5)
    wait_sent(stat_land.at[pl.ds(0, HEADS - 1)], 6)
    wait_sent(ny_send.at[pl.ds(0, HEADS - 1)], 7)
    wait_sent(sib_send, 8)
    wait_sent(dkv_send.at[pl.ds(0, HEADS - 1)], 9)
    wait_sent(dq_send.at[pl.ds(0, HEADS - 1)], 13)
    wait_sent(w_sib_send, 18)

    @pl.when(owns_w)
    def _():
        wait_sent(w_send.at[pl.ds(0, 15)], 10)
        wait_sent(w_land.at[pl.ds(0, N_SEQ - 1)], 12)

    @pl.when(jnp.logical_not(owns_w))
    def _():
        wait_sent(w_send, 10)

    wait_sent(dx_send.at[pl.ds(0, 15)], 11)
    wait_sent(dx_send.at[pl.ds(0, 16)], 16)
    wait_sent(col_send.at[0, pl.ds(0, N_SEQ - 1)], 15)
    wait_sent(col_send.at[1, pl.ds(0, N_SEQ - 1)], 17)


def on_device(table, item_rows, lengths, w_in, w_out, cotangent):
    vmem = pl.BlockSpec(memory_space=pltpu.VMEM)
    smem = pl.BlockSpec(memory_space=pltpu.SMEM)
    anywhere = pl.BlockSpec(memory_space=pl.ANY)
    buf = pltpu.VMEM
    scratch = [
        buf((ROWS_T, WIDTH), BF16),
        buf((WIDTH, 4 * WIDTH), BF16),
        buf((WIDTH, WIDTH), BF16),
        buf((EVENTS, WIDTH), BF16),
        buf((1, EVENTS), I32),
        buf((N_TABLE, 1, EVENTS), I32),
        buf((N_TABLE, 16, 256), BF16),
        buf((N_TABLE, 16, 256), BF16),
        buf((8, 128), F32),
        buf((N_SEQ, 8, 128), F32),
        buf((HEADS, 128, 128), BF16),
        buf((HEADS, 128, 128), BF16),
        buf((HEADS, HEAD, 128), BF16),
        buf((HEADS, HEAD, 128), BF16),
        buf((HEADS, 128, 128), BF16),
        buf((HEADS, HEAD, 128), BF16),
        buf((HEADS, HEAD, 128), BF16),
        buf((24, 128), F32),
        buf((HEADS, 24, 128), F32),
        buf((HEADS, HEAD, 128), BF16),
        buf((HEADS, HEAD, 128), BF16),
        buf((N_TABLE, 16, WIDTH), F32),
        buf((16, 16, WIDTH), BF16),
        buf((16, 16, WIDTH), BF16),
        buf((16, 16, WIDTH), BF16),
        buf((N_TABLE, 16, WIDTH), BF16),
        buf((16, WIDTH), BF16),
        buf((HEADS, 16, WIDTH), BF16),
        buf((HEADS, 128, 128), BF16),
        buf((HEADS, 128, 128), BF16),
        buf((HEADS, 128, 128), BF16),
        buf((HEADS, 128, 128), BF16),
        buf((HEADS, HEAD, 128), BF16),
        buf((HEADS, HEAD, 128), BF16),
        buf((N_TABLE, 16, 256), BF16),
        buf((N_TABLE, 16, 256), BF16),
        buf((2, N_SEQ, 32, 128), BF16),
        buf((2, N_SEQ, 32, 128), BF16),
        buf((EVENTS, WIDTH), F32),
        buf((WIDTH, EVENTS), F32),
        buf((WIDTH, EVENTS), F32),
        buf((EVENTS, WIDTH), F32),
        buf((EVENTS, 4 * WIDTH), F32),
        buf((2048, 128), BF16),
        buf((4, 128, 512), BF16),
        buf((1024, 128), BF16),
        buf((1024, 128), BF16),
        buf((10, 512, 256), BF16),
        buf((10, 512, 256), F32),
        buf((8, HEAD, 128), F32),
        buf((4, HEAD, 256), F32),
        buf((2048, 128), F32),
        buf((8, N_SEQ // 4, 256, 128), BF16),
        buf((8, N_SEQ * 32, 128), F32),
        buf((SLOTS, 128), F32),
        pltpu.SemaphoreType.DMA((5,)),
        pltpu.SemaphoreType.DMA((19,)),
        pltpu.SemaphoreType.DMA((19,)),
        pltpu.SemaphoreType.DMA((HEADS,)),
        pltpu.SemaphoreType.DMA((2,)),
    ]
    sums, w_grad = pl.pallas_call(
        kernel,
        out_shape=(
            pltpu.VMEM((32, ROWS_T), F32),
            pltpu.VMEM((16, WIDTH), F32),
        ),
        in_specs=[anywhere, smem, anywhere, anywhere, anywhere, anywhere],
        out_specs=(vmem, vmem),
        scratch_shapes=scratch,
        compiler_params=pltpu.CompilerParams(
            collective_id=0, has_side_effects=True, vmem_limit_bytes=56 * 1024 * 1024
        ),
    )(item_rows, lengths, cotangent[0], table, w_in, w_out)
    return sums.T, w_grad


def solution(mesh):
    return jax.shard_map(
        on_device,
        mesh=mesh,
        in_specs=(
            P("table", None),
            P("table", "seq"),
            P("table"),
            P(),
            P(),
            P("table", "seq", None),
        ),
        out_specs=(P("table", "seq"), P("table", None)),
        check_vma=False,
    )
```
